256 devices in a mesh: sub: 8 (over y, core), dev: 32 (over z, x).
Axes of the slice: x: 4, y: 4, z: 8, core: 2. Of those that a mesh axis runs over, the one named last changes fastest.
Arguments:
- load: float32 [262144, 256], P(('sub', 'dev')), may hold values from -6 to 6
- schur: bfloat16 [262144, 1024], P(('sub', 'dev')), as said below
- local_inverse: bfloat16 [262144, 1024], P(('sub', 'dev')), as said below
- coarse_basis: float32 [4096, 1024], P(('sub', 'dev')), may hold values from -0.1875 to 0.1875
- coarse_inverse: float32 [1024, 1024], P('dev'), as said below
- dof_lists: int32 [256, 4, 256], P(('sub', 'dev')), may hold values from -1 to 1023, as said below
- coarse_map: int32 [256, 16], P(('sub', 'dev')), may hold values from 0 to 1023, as said below
- stiffness: float32 [256], replicated, may hold values from 1 to 1000
Outputs:
- solution: float32 [262144, 256], P(('sub', 'dev'))
- residual: float32 [262144, 256], P(('sub', 'dev'))
The draws below stay inside these ranges and needn't reach their ends.
Inputs may be any that keep to these rules, and one draw needn't show every extreme that they name: dof_lists[p, k, j] for j below that pair's count names the local unknown of subdomain p that is the j-th one shared with its neighbour in direction k, and -1 past the count; the entry of the neighbour in the opposite direction at the same j names the same unknown. The named entries of a subdomain are exactly 0 to its count minus one, each once; directions without a neighbour are all -1; one pair shares 256 unknowns and one subdomain has 1024. `coarse_map`: distinct within a subdomain; every coarse unknown is named by exactly four primal unknowns in all. `schur`: each block is symmetric positive definite. `local_inverse`: each block is symmetric positive definite. `coarse_inverse`: symmetric positive definite.
All inputs are finite; a program needn't handle non-finite values.
Results may differ from the reference program's by a relative error of at most 0.0093.
Values sent between devices are 32-bit elements; how exact they have to be, the bound alone decides.
No kernel may reach another device: no remote copies, remote signals or barrier semaphores. Data moves between devices by JAX's collectives and lax.ppermute only.
A program may use at most 64 MiB of HBM per device.

```python
import math
import jax
import jax.numpy as jnp
from jax import lax

NI = 1024
NRHS = 256
NCL = 16
ITERS = 2
CAP = 256
NC = 1024
N_SUB = 8
N_DEV = 32
DEVICES = 256


def symmetric_block(key, unknowns, share, lowest, largest_value):
    first, second = jax.random.split(key)
    raw = jax.random.uniform(first, (unknowns, unknowns), jnp.float32, -1.0, 1.0)
    off_part = (raw + raw.T) * (share * lowest * 1.2247449 / math.sqrt(unknowns))
    diagonal = jax.random.uniform(second, (unknowns,), jnp.float32, lowest, largest_value)
    identity = jnp.eye(unknowns, dtype=jnp.float32)
    return off_part * (1.0 - identity) + identity * diagonal[None, :]


def draw_schur(key, part):
    key = jax.random.fold_in(key, 31)
    keys = jax.random.split(key, DEVICES)
    blocks = lax.map(lambda single: symmetric_block(single, NI, 0.3, 2.0, 4.0), keys)
    return blocks.reshape(DEVICES * NI, NI).astype(jnp.bfloat16)


def draw_local_inverse(key, part):
    key = jax.random.fold_in(key, 37)
    keys = jax.random.split(key, DEVICES)
    blocks = lax.map(lambda single: symmetric_block(single, NI, 0.3, 0.25, 0.5), keys)
    return blocks.reshape(DEVICES * NI, NI).astype(jnp.bfloat16)


def draw_coarse_inverse(key, part):
    key = jax.random.fold_in(key, 41)
    return symmetric_block(key, NC, 0.3, 0.5, 1.0)


def draw_dof_lists(key, part):
    key = jax.random.fold_in(key, 11)
    keys = jax.random.split(key, 5)
    lowest = max(CAP // 8, 1)
    largest_value = CAP // 2
    sub_pairs = jax.random.randint(keys[0], (N_SUB - 1, N_DEV), lowest, largest_value + 1)
    dev_pairs = jax.random.randint(keys[1], (N_SUB, N_DEV - 1), lowest, largest_value + 1)
    heavy_sub = jax.random.randint(keys[2], (), 1, N_SUB - 1)
    heavy_dev = jax.random.randint(keys[3], (), 1, N_DEV - 1)
    pair_rows = jnp.arange(N_SUB - 1, dtype=jnp.int32)[:, None]
    pair_cols = jnp.arange(N_DEV, dtype=jnp.int32)[None, :]
    sub_pairs = jnp.where(((pair_rows == heavy_sub) | (pair_rows == heavy_sub - 1)) & (pair_cols == heavy_dev), CAP, sub_pairs)
    grid_rows = jnp.arange(N_SUB, dtype=jnp.int32)[:, None]
    edge_cols = jnp.arange(N_DEV - 1, dtype=jnp.int32)[None, :]
    dev_pairs = jnp.where((grid_rows == heavy_sub) & ((edge_cols == heavy_dev) | (edge_cols == heavy_dev - 1)), CAP, dev_pairs)
    zero_row = jnp.zeros((1, N_DEV), jnp.int32)
    zero_col = jnp.zeros((N_SUB, 1), jnp.int32)
    counts = jnp.stack([jnp.concatenate([zero_row, sub_pairs], axis=0), jnp.concatenate([sub_pairs, zero_row], axis=0), jnp.concatenate([zero_col, dev_pairs], axis=1), jnp.concatenate([dev_pairs, zero_col], axis=1)], axis=-1).reshape(DEVICES, 4).astype(jnp.int32)
    offsets = jnp.cumsum(counts, axis=1) - counts
    totals = jnp.sum(counts, axis=1)
    position = jnp.arange(NI, dtype=jnp.int32)[None, :]
    scores = jax.random.randint(keys[4], (DEVICES, NI), 0, 2 ** 19) * NI + position
    scores = jnp.where(position < totals[:, None], scores, 2 ** 30 + position)
    ordering = jnp.argsort(scores, axis=1, stable=True).astype(jnp.int32)
    within = jnp.arange(CAP, dtype=jnp.int32)[None, None, :]
    where_at = jnp.clip(offsets[:, :, None] + within, 0, NI - 1)
    entries = ordering[jnp.arange(DEVICES, dtype=jnp.int32)[:, None, None], where_at]
    return jnp.where(within < counts[:, :, None], entries, -1).astype(jnp.int32)


def draw_coarse_map(key, part):
    key = jax.random.fold_in(key, 23)
    scores = jax.random.randint(key, (4, NC), 0, 2 ** 20) * NC + jnp.arange(NC, dtype=jnp.int32)[None, :]
    ordering = jnp.argsort(scores, axis=1, stable=True).astype(jnp.int32)
    return ordering.reshape(DEVICES, NCL).astype(jnp.int32)


def level_of(key, shape, pieces, low, high):
    level, own = 1.0, jax.random.fold_in(key, 6)
    for dim, blocks in pieces:
        draws = jnp.exp(jax.random.uniform(jax.random.fold_in(own, dim), (blocks,), jnp.float32, low / len(pieces), high / len(pieces)))
        level = level * jnp.repeat(draws, shape[dim] // blocks).reshape([-1 if axis == dim else 1 for axis in range(len(shape))])
    return level


def normal_values(rng, extent, spread, reach, shards=(), kind=jnp.bfloat16):
    values = jax.random.normal(rng, extent, jnp.float32) * spread
    if len(shards) > 0:
        values = level_of(rng, extent, shards, -0.22, 0.18) * values
    return jnp.clip(values, min=-reach, max=reach).astype(kind)


def setup_inputs(seed: int = 0) -> dict:
    key_list = jax.random.split(jax.random.key(seed), 9)
    return {
        "load": normal_values(key_list[0], (DEVICES * NI, NRHS), 1.0, 6.0, ((0, 256),), jnp.float32),
        "schur": draw_schur(jax.random.fold_in(key_list[8], 71), 0),
        "local_inverse": draw_local_inverse(jax.random.fold_in(key_list[8], 71), 0),
        "coarse_basis": normal_values(key_list[3], (DEVICES * NCL, NI), NI ** -0.5, 0.1875, ((0, 256),), jnp.float32),
        "coarse_inverse": draw_coarse_inverse(jax.random.fold_in(key_list[8], 71), 0),
        "dof_lists": draw_dof_lists(jax.random.fold_in(key_list[8], 71), 0),
        "coarse_map": draw_coarse_map(jax.random.fold_in(key_list[8], 71), 0),
        "stiffness": jnp.clip(jnp.exp(jax.random.uniform(key_list[7], (DEVICES,), jnp.float32, math.log(1.0), math.log(1000.0))), 1.0, 1000.0),
    }


def reference(load, schur, local_inverse, coarse_basis, coarse_inverse, dof_lists, coarse_map, stiffness):
    largest_value = lax.Precision.HIGHEST
    subdomain = jnp.arange(DEVICES, dtype=jnp.int32)
    in_use = dof_lists >= 0
    live_count = jnp.sum(in_use.astype(jnp.int32), axis=(1, 2))
    active_mask = (jnp.arange(NI, dtype=jnp.int32)[None, :] < live_count[:, None]).astype(jnp.float32)[:, :, None]
    sub_index = subdomain // N_DEV
    dev_index = subdomain % N_DEV
    shifts = jnp.array([-N_DEV, N_DEV, -1, 1], dtype=jnp.int32)
    neighbours = jnp.clip(subdomain[:, None] + shifts[None, :], 0, DEVICES - 1).astype(jnp.int32)
    present = jnp.stack([sub_index > 0, sub_index < N_SUB - 1, dev_index > 0, dev_index < N_DEV - 1], axis=1).astype(jnp.float32)
    slot_weight = stiffness[:, None] / (stiffness[:, None] + stiffness[neighbours])
    target = jnp.where(in_use, dof_lists, NI).astype(jnp.int32)
    safe_rows = jnp.where(in_use, dof_lists, 0).astype(jnp.int32)
    rows_index = subdomain[:, None, None]
    weights = jnp.zeros((DEVICES, NI + 1), jnp.float32).at[rows_index, target].set(
        jnp.broadcast_to(slot_weight[:, :, None], dof_lists.shape).astype(jnp.float32))[:, :NI, None]
    opposite = jnp.array([1, 0, 3, 2], dtype=jnp.int32)
    in_use_float = in_use.astype(jnp.float32)[..., None]

    def assemble(values):
        packed = values[rows_index, safe_rows] * in_use_float
        incoming = packed[neighbours, opposite[None, :]] * present[:, :, None, None]
        padded = jnp.concatenate([values, jnp.zeros((DEVICES, 1, values.shape[2]), jnp.float32)], axis=1)
        return padded.at[rows_index, target].add(incoming)[:, :NI]

    matrices = schur.reshape(DEVICES, NI, NI)
    inverses = local_inverse.reshape(DEVICES, NI, NI)
    coarse_basis_row_set = coarse_basis.reshape(DEVICES, NCL, NI)

    def apply_blocks(blocks, vectors):
        return lax.map(lambda operands: jnp.dot(operands[0], operands[1], preferred_element_type=jnp.float32),
                       (blocks, vectors.astype(jnp.bfloat16)))

    def coarse_sum(weighted_vector):
        projected_vector = jnp.einsum("gzm,gmn->gzn", coarse_basis_row_set, weighted_vector, precision=largest_value)
        return jnp.zeros((NC, NRHS), jnp.float32).at[coarse_map.reshape(-1)].add(projected_vector.reshape(-1, NRHS))

    def precondition(residual, coarse_rhs):
        weighted_vector = weights * residual
        local_part = active_mask * apply_blocks(inverses, weighted_vector)
        solved = jnp.dot(coarse_inverse, coarse_rhs, precision=largest_value)
        selected_entries = solved[coarse_map]
        coarse_correction_term = active_mask * jnp.einsum("mzf,mzl->mfl", coarse_basis_row_set, selected_entries, precision=largest_value)
        return assemble(weights * (local_part + coarse_correction_term))

    def weighted_dot(left, right):
        return jnp.sum(weights * left * right, axis=(0, 1))

    values = load.reshape(DEVICES, NI, NRHS)
    residual = assemble(active_mask * values)
    coarse_rhs = coarse_sum(weights * residual)
    precond = precondition(residual, coarse_rhs)
    norm_now = weighted_dot(residual, precond)
    direction = precond
    solution = jnp.zeros_like(residual)
    for iteration in range(ITERS):
        applied = assemble(active_mask * apply_blocks(matrices, direction))
        step_size = norm_now / weighted_dot(direction, applied)
        solution = solution + step_size * direction
        residual = residual - step_size * applied
        if iteration + 1 < ITERS:
            coarse_rhs = coarse_sum(weights * residual)
            precond = precondition(residual, coarse_rhs)
            norm_next = weighted_dot(residual, precond)
            direction = precond + (norm_next / norm_now) * direction
            norm_now = norm_next
    return solution.reshape(DEVICES * NI, NRHS), residual.reshape(DEVICES * NI, NRHS)
```

```python
import jax
import jax.numpy as jnp
import numpy as np
from jax import lax
from jax.experimental import pallas as pl
from jax.experimental.pallas import tpu as pltpu
from jax.sharding import PartitionSpec as P

F32, BF16 = jnp.float32, jnp.bfloat16
EXACT = lax.Precision.HIGHEST
NI, NRHS, NCL, CAP, NC = 1024, 256, 16, 256, 1024
N_SUB, N_DEV, N_X, N_Z = 8, 32, 4, 8
PEERS = N_SUB * N_X
MIB = 1 << 20
NN = (((1,), (0,)), ((), ()))
NT = (((1,), (1,)), ((), ()))


def mm(a, b, dims=NN, precision=None):
    return lax.dot_general(a, b, dims, precision=precision, preferred_element_type=F32)


def pieces(v, count):
    out = []
    for i in range(count):
        part = v.astype(BF16)
        out.append(part)
        if i + 1 < count:
            v = v - part.astype(F32)
    return out


def shape(*dims, dtype=F32):
    return jax.ShapeDtypeStruct(dims, dtype)


def run(body, outs, ins, smem=(), scratch=(), limit=40, flops=0):
    vmem = pl.BlockSpec(memory_space=pltpu.VMEM)
    specs = [pl.BlockSpec(memory_space=pltpu.SMEM) if i in smem else vmem for i in range(len(ins))]
    size = sum(int(np.prod(a.shape)) * a.dtype.itemsize for a in list(ins) + list(outs))
    return pl.pallas_call(
        body,
        out_shape=list(outs),
        in_specs=specs,
        out_specs=[vmem] * len(outs),
        scratch_shapes=list(scratch),
        compiler_params=pltpu.CompilerParams(vmem_limit_bytes=limit * MIB),
        cost_estimate=pl.CostEstimate(flops=flops, bytes_accessed=size, transcendentals=0),
        name=body.__name__,
    )(*ins)


def slot_weights(me, stiffness):
    s, d = me[0], me[1]
    p = s * N_DEV + d
    own = jnp.full((1, NRHS), stiffness[p], F32)
    out = []
    for shift in (-N_DEV, N_DEV, -1, 1):
        q = jnp.clip(p + shift, 0, N_SUB * N_DEV - 1)
        out.append(own / (own + jnp.full((1, NRHS), stiffness[q], F32)))
    return out


def iota(dims, axis):
    return lax.broadcasted_iota(jnp.int32, dims, axis)


def slot_major(dof):
    wide = jnp.concatenate([dof.astype(F32), jnp.zeros((4, CAP), F32)], axis=0)
    columns = jnp.transpose(wide)
    lanes = iota((CAP, NI), 1).astype(F32)
    return [jnp.where(columns[:, k : k + 1] == lanes, 1.0, 0.0).astype(BF16) for k in range(4)]


def unknown_major(dof):
    rows = iota((NI, CAP), 0)
    return [jnp.where(rows == dof[k : k + 1, :], 1.0, 0.0).astype(BF16) for k in range(4)]


def rows_of(k):
    return slice(k * CAP, (k + 1) * CAP)


HROWS = CAP + NCL + 8


def prepare(me, stiffness, dof, load, basis, names, h0, h1, h2, h3, wide, perm):
    for k, block in enumerate(slot_major(dof[...])):
        perm[rows_of(k), :] = block
    for i, part in enumerate(pieces(load[...], 3)):
        wide[:, i * NRHS : (i + 1) * NRHS] = part
    basis_parts = jnp.concatenate(pieces(basis[...], 3), axis=0)
    weights = slot_weights(me, stiffness)
    for k, h in enumerate((h0, h1, h2, h3)):
        both = mm(perm[rows_of(k), :], wide[...])
        h[0:CAP, :] = both[:, :NRHS] + both[:, NRHS : 2 * NRHS] + both[:, 2 * NRHS :]
        three = mm(basis_parts, perm[rows_of(k), :], NT)
        h[CAP : CAP + NCL, :] = weights[k] * (
            three[:NCL] + three[NCL : 2 * NCL] + three[2 * NCL :]
        )
        h[CAP + NCL :, :] = jnp.concatenate([names[...], names[...]], axis=1)


def permute_blocks(dof, schur, inverse, schur_out, inverse_out, perm, perm_t, half):
    for k, block in enumerate(slot_major(dof[...])):
        perm[rows_of(k), :] = block
    for k, block in enumerate(unknown_major(dof[...])):
        perm_t[:, rows_of(k)] = block
    for source, target in ((inverse, inverse_out), (schur, schur_out)):
        for k in range(4):
            half[rows_of(k), :] = mm(perm[rows_of(k), :], source[...]).astype(BF16)
        for k in range(4):
            target[rows_of(k), :] = mm(half[rows_of(k), :], perm_t[...]).astype(BF16)


def block_product(matrix, wide, k):
    both = mm(matrix[rows_of(k), :], wide[...])
    return both[:, :NRHS] + both[:, NRHS:]


def split_into(wide, k, v):
    for i, part in enumerate(pieces(v, 2)):
        wide[rows_of(k), i * NRHS : (i + 1) * NRHS] = part


def lane_slot(j):
    return lax.div(iota((8, 128), 1), NCL) == j


def begin(
    me, stiffness, inverse, h0, h1, h2, h3, g0, g1, g2, g3,
    send, rows_out, columns_out, r_out, e0, e1, e2, e3, wide,
):
    hs, gs, es = (h0, h1, h2, h3), (g0, g1, g2, g3), (e0, e1, e2, e3)
    s, d = me[0], me[1]
    x = lax.rem(d, N_X)
    odd = lax.rem(s, 2)
    own = odd * 4 + x
    across, over, edge = (
        (1 - odd) * 4 + x,
        (1 - odd) * 4 + lax.rem(x + 1, 4),
        (1 - odd) * 4 + lax.rem(x + 2, 4),
    )
    places = (
        jnp.where(odd == 1, across, over),
        jnp.where(odd == 1, over, across),
        jnp.where(x > 0, odd * 4 + x - 1, edge),
        jnp.where(x < N_X - 1, odd * 4 + x + 1, edge),
    )
    weights = slot_weights(me, stiffness)
    rows_out[...] = jnp.zeros_like(rows_out)
    total = jnp.zeros((128, NRHS), F32)
    for k in range(4):
        rows_out[pl.ds(pl.multiple_of(own * NCL, NCL), NCL), rows_of(k)] = hs[k][CAP : CAP + NCL, :]
        rows_out[pl.ds(pl.multiple_of(places[k] * NCL, NCL), NCL), rows_of(k)] = gs[k][
            CAP : CAP + NCL, :
        ]
        total = total + mm(rows_out[:, rows_of(k)], hs[k][0:CAP, :], precision=EXACT)
    columns_out[...] = jnp.transpose(rows_out[...])
    flipped = jnp.transpose(total)
    zero = jnp.zeros((8, 128), F32)
    line = iota((8, 128), 0)
    mine = jnp.where(lane_slot(own), hs[0][CAP + NCL :, 0:128], zero)
    before = jnp.where(lane_slot(s) & (x == 0), gs[2][CAP + NCL :, 0:128], zero)
    after = jnp.where(lane_slot(s) & (x == N_X - 1), gs[3][CAP + NCL :, 0:128], zero)
    extra = jnp.where(line == 0, mine, jnp.where(line == 1, before, jnp.where(line == 2, after, zero)))
    for m in range(PEERS):
        send[m * 16 : m * 16 + 8, :] = flipped[m * 8 : m * 8 + 8, :]
        send[m * 16 + 8 : m * 16 + 16, :] = extra
    for k in range(4):
        r = hs[k][0:CAP, :] + gs[k][0:CAP, :]
        r_out[rows_of(k), :] = r
        split_into(wide, k, weights[k] * r)
    for k in range(4):
        es[k][...] = weights[k] * block_product(inverse, wide, k)


def layout(m):
    s, x = divmod(m, N_X)
    odd = s % 2
    keep = [odd * 4 + x, (1 - odd) * 4 + x]
    keep += [odd * 4 + v for v in (x - 1, x + 1) if 0 <= v < N_X]
    moves = []
    other = s + 1 if odd else s - 1
    if 0 <= other < N_SUB:
        moves.append(((1 - odd) * 4 + (x + 1) % 4, other // 2, (1 - odd) * 4 + x))
    if x in (0, N_X - 1):
        moves.append(((1 - odd) * 4 + (x + 2) % 4, 4 if x == 0 else 5, s))
    return s // 2, keep, moves


def lanes_in(slots):
    at = lax.div(iota((8, 128), 1), NCL)
    hit = at == slots[0]
    for j in slots[1:]:
        hit = hit | (at == j)
    return hit


def roll_slots(v, shift):
    shift = (shift * NCL) % 128
    return pltpu.roll(v, shift, 1) if shift else v


def spread(tiles):
    groups = [jnp.zeros((8, 128), F32) for _ in range(6)]
    for m in range(PEERS):
        base, keep, moves = layout(m)
        tile = tiles(m)
        groups[base] = groups[base] + jnp.where(lanes_in(keep), tile, 0.0)
        for here, group, there in moves:
            part = roll_slots(jnp.where(lanes_in([here]), tile, 0.0), there - here)
            groups[group] = groups[group] + part
    return jnp.concatenate(groups, axis=1)


def fold(groups, pick, out):
    three = mm(jnp.concatenate(pieces(groups, 3), axis=0), pick, NT)
    result = three[0:8] + three[8:16] + three[16:24]
    for z in range(N_Z):
        out[z * 8 : z * 8 + 8, :] = result


def gather_first(received, out, pick_out):
    groups = spread(lambda m: received[m * 16 : m * 16 + 8, :])
    ids = [jnp.zeros((8, 128), F32) for _ in range(6)]
    for m in range(PEERS):
        extra = received[m * 16 + 8 : m * 16 + 16, :]
        base = m // 8
        ids[base] = ids[base] + extra
        ids[4] = ids[4] + extra
        ids[5] = ids[5] + extra
    index = jnp.concatenate(
        [ids[0][0:1], ids[1][0:1], ids[2][0:1], ids[3][0:1], ids[4][1:2], ids[5][2:3]], axis=1
    ).astype(jnp.int32)
    pick = jnp.where(iota((NC, 768), 0) == index, 1.0, 0.0).astype(BF16)
    pick_out[...] = pick
    fold(groups, pick, out)


def gather_again(received, pick, out):
    fold(spread(lambda m: received[m * 8 : m * 8 + 8, :]), pick[...], out)


def coarse_solve(me, received, k0, k1, k2, k3, out, rows):
    x = lax.rem(me[1], N_X)
    for i, block in enumerate((k0, k1, k2, k3)):
        at = lax.rem(x + (N_X - i), N_X) * 32
        rows[pl.ds(pl.multiple_of(at, 32), 32), :] = block[...]
    rhs = received[0:8, :]
    for z in range(1, N_Z):
        rhs = rhs + received[z * 8 : z * 8 + 8, :]
    solved = mm(rhs, rows[...], NT, precision=EXACT)
    for z in range(N_Z):
        out[z * 8 : z * 8 + 8, :] = solved


def give_back(received, pick, out):
    solved = jnp.concatenate([received[z * 8 : z * 8 + 8, :] for z in range(N_Z)], axis=1)
    three = mm(jnp.concatenate(pieces(solved, 3), axis=0), pick[...])
    every = three[0:8] + three[8:16] + three[16:24]
    groups = [every[:, g * 128 : (g + 1) * 128] for g in range(6)]
    for m in range(PEERS):
        base, keep, moves = layout(m)
        tile = jnp.where(lanes_in(keep), groups[base], 0.0)
        for here, group, there in moves:
            tile = jnp.where(lanes_in([here]), roll_slots(groups[group], here - there), tile)
        out[m * 8 : m * 8 + 8, :] = tile


def first_direction(
    schur, rows, columns, me, stiffness, solved, r, e0, e1, e2, e3, g0, g1, g2, g3,
    send, p_out, dots, q0, q1, q2, q3, wide,
):
    weights = slot_weights(me, stiffness)
    norm = jnp.zeros((1, NRHS), F32)
    curvature = jnp.zeros((1, NRHS), F32)
    total = jnp.zeros((128, NRHS), F32)
    for k, (e, g) in enumerate(zip((e0, e1, e2, e3), (g0, g1, g2, g3))):
        p = e[...] + g[...] + mm(columns[rows_of(k), :], solved[...], NT, precision=EXACT)
        p_out[rows_of(k), :] = p
        norm = norm + weights[k] * jnp.sum(r[rows_of(k), :] * p, axis=0, keepdims=True)
        split_into(wide, k, p)
    for k, q in enumerate((q0, q1, q2, q3)):
        value = block_product(schur, wide, k)
        q[...] = value
        curvature = curvature + jnp.sum(value * p_out[rows_of(k), :], axis=0, keepdims=True)
        total = total + mm(rows[:, rows_of(k)], value, precision=EXACT)
    send[...] = jnp.transpose(total)
    dots[0:1, :] = norm
    dots[1:2, :] = curvature


def second_local(
    inverse, me, stiffness, q0, q1, q2, q3, g0, g1, g2, g3, t_out, e0, e1, e2, e3, wide
):
    weights = slot_weights(me, stiffness)
    for k, (q, g) in enumerate(zip((q0, q1, q2, q3), (g0, g1, g2, g3))):
        t = q[...] + g[...]
        t_out[rows_of(k), :] = t
        split_into(wide, k, weights[k] * t)
    for k, e in enumerate((e0, e1, e2, e3)):
        e[...] = weights[k] * block_product(inverse, wide, k)


def second_direction(
    schur, columns, me, stiffness, solved, dots, t, e0, e1, e2, e3, g0, g1, g2, g3,
    send, v_out, u0, u1, u2, u3, wide,
):
    weights = slot_weights(me, stiffness)
    first = jnp.zeros((1, NRHS), F32)
    second = jnp.zeros((1, NRHS), F32)
    for k, (e, g) in enumerate(zip((e0, e1, e2, e3), (g0, g1, g2, g3))):
        v = e[...] + g[...] + mm(columns[rows_of(k), :], solved[...], NT, precision=EXACT)
        v_out[rows_of(k), :] = v
        first = first + weights[k] * jnp.sum(t[rows_of(k), :] * v, axis=0, keepdims=True)
        split_into(wide, k, v)
    for k, u in enumerate((u0, u1, u2, u3)):
        value = block_product(schur, wide, k)
        u[...] = value
        second = second + jnp.sum(value * v_out[rows_of(k), :], axis=0, keepdims=True)
    values = (dots[0:1, :], dots[1:2, :], first, second)
    tile = jnp.concatenate([v[:, :128] for v in values] + [v[:, 128:] for v in values], axis=0)
    for m in range(PEERS):
        send[m * 8 : m * 8 + 8, :] = tile


def add_plane(received, out):
    total = received[0:8, :]
    for m in range(1, PEERS):
        total = total + received[m * 8 : m * 8 + 8, :]
    for z in range(N_Z):
        out[z * 8 : z * 8 + 8, :] = total


def finish(
    received, dof, r, p, t, v, u0, u1, u2, u3, g0, g1, g2, g3, x_out, r_out, perm_t, wide
):
    total = received[0:8, :]
    for z in range(1, N_Z):
        total = total + received[z * 8 : z * 8 + 8, :]
    norm, curvature, g, h = (
        jnp.concatenate([total[i : i + 1], total[i + 4 : i + 5]], axis=1) for i in range(4)
    )
    step = norm / curvature
    scaled = step * g
    grown = scaled / curvature
    next_norm = (grown - 1.0) * norm
    next_curvature = step * (step * h) - grown * scaled
    next_step = next_norm / next_curvature
    for k, (u, halo) in enumerate(zip((u0, u1, u2, u3), (g0, g1, g2, g3))):
        rows = rows_of(k)
        w = u[...] + halo[...]
        both = step + next_step * grown
        solution = both * p[rows, :] - (next_step * step) * v[rows, :]
        residual = r[rows, :] - both * t[rows, :] + (next_step * step) * w
        for i, part in enumerate(pieces(solution, 3)):
            wide[rows, i * NRHS : (i + 1) * NRHS] = part
        for i, part in enumerate(pieces(residual, 3)):
            wide[rows, (i + 3) * NRHS : (i + 4) * NRHS] = part
    for k, block in enumerate(unknown_major(dof[...])):
        perm_t[:, rows_of(k)] = block
    for k in range(4):
        rows = rows_of(k)
        for j, out in enumerate((x_out, r_out)):
            three = mm(perm_t[rows, :], wide[:, 3 * j * NRHS : 3 * (j + 1) * NRHS])
            out[rows, :] = three[:, :NRHS] + three[:, NRHS : 2 * NRHS] + three[:, 2 * NRHS :]


PLANES = [[s * N_DEV + z * N_X + x for s in range(N_SUB) for x in range(N_X)] for z in range(N_Z)]
LINES = [[z * N_X + x for z in range(N_Z)] for x in range(N_X)]


def over_plane(v):
    return lax.all_to_all(v, ("sub", "dev"), 0, 0, tiled=True, axis_index_groups=PLANES)


def over_line(v):
    return lax.all_to_all(v, "dev", 0, 0, tiled=True, axis_index_groups=LINES)


def ring(v, axis, count, shift):
    return lax.ppermute(v, axis, [(i, (i + shift) % count) for i in range(count)])


def halo(blocks):
    return [
        ring(blocks[1], "sub", N_SUB, 1),
        ring(blocks[0], "sub", N_SUB, -1),
        ring(blocks[3], "dev", N_DEV, 1),
        ring(blocks[2], "dev", N_DEV, -1),
    ]


def shards(
    load, schur, local_inverse, coarse_basis, coarse_inverse, dof_lists, coarse_map, stiffness
):
    me = jnp.stack([lax.axis_index("sub"), lax.axis_index("dev")]).astype(jnp.int32)
    dof = dof_lists[0]
    names = jnp.broadcast_to(jnp.tile(coarse_map, (1, 8)).astype(F32), (8, 128))
    block = shape(CAP, NRHS)
    vector = shape(NI, NRHS)
    square = shape(NI, NI, dtype=BF16)
    wide = pltpu.VMEM((NI, 2 * NRHS), BF16)
    big = 2 * NI * NI * NRHS

    hs = run(
        prepare,
        [shape(HROWS, NRHS)] * 4,
        [me, stiffness, dof, load, coarse_basis, names],
        smem=(0, 1),
        scratch=[pltpu.VMEM((NI, 3 * NRHS), BF16), pltpu.VMEM((NI, NI), BF16)],
        flops=3 * big,
    )
    gs = halo(hs)
    planes = [coarse_inverse] + [
        lax.ppermute(
            coarse_inverse,
            "dev",
            [(z * N_X + x, z * N_X + (x + i) % N_X) for z in range(N_Z) for x in range(N_X)],
        )
        for i in range(1, N_X)
    ]
    schur_s, inverse_s = run(
        permute_blocks,
        [square, square],
        [dof, schur, local_inverse],
        scratch=[pltpu.VMEM((NI, NI), BF16)] * 3,
        flops=16 * big,
    )
    send, rows, columns, r, *es = run(
        begin,
        [shape(PEERS * 16, 128), shape(128, NI), shape(NI, 128), vector] + [block] * 4,
        [me, stiffness, inverse_s, *hs, *gs],
        smem=(0, 1),
        scratch=[wide],
        flops=2 * big,
    )
    es_halo = halo(es)
    line, pick = run(
        gather_first,
        [shape(N_Z * 8, NC), shape(NC, 768, dtype=BF16)],
        [over_plane(send)],
    )

    def coarse_tail(line):
        (part,) = run(
            coarse_solve,
            [shape(N_Z * 8, 128)],
            [me, over_line(line), *planes],
            smem=(0,),
            scratch=[pltpu.VMEM((128, NC), F32)],
        )
        (back,) = run(give_back, [shape(PEERS * 8, 128)], [over_line(part), pick])
        return over_plane(back)

    solved = coarse_tail(line)
    send, p, dots, *qs = run(
        first_direction,
        [shape(PEERS * 8, 128), vector, shape(8, NRHS)] + [block] * 4,
        [schur_s, rows, columns, me, stiffness, solved, r, *es, *es_halo],
        smem=(3, 4),
        scratch=[wide],
        flops=2 * big,
    )
    qs_halo = halo(qs)
    (line,) = run(gather_again, [shape(N_Z * 8, NC)], [over_plane(send), pick])
    t, *es = run(
        second_local,
        [vector] + [block] * 4,
        [inverse_s, me, stiffness, *qs, *qs_halo],
        smem=(1, 2),
        scratch=[wide],
        flops=2 * big,
    )
    es_halo = halo(es)
    solved = coarse_tail(line)
    send, v, *us = run(
        second_direction,
        [shape(PEERS * 8, 128), vector] + [block] * 4,
        [schur_s, columns, me, stiffness, solved, dots, t, *es, *es_halo],
        smem=(2, 3),
        scratch=[wide],
        flops=2 * big,
    )
    us_halo = halo(us)
    (line,) = run(add_plane, [shape(N_Z * 8, 128)], [over_plane(send)])
    return tuple(
        run(
            finish,
            [vector, vector],
            [over_line(line), dof, r, p, t, v, *us, *us_halo],
            scratch=[pltpu.VMEM((NI, NI), BF16), pltpu.VMEM((NI, 6 * NRHS), BF16)],
            flops=6 * big,
        )
    )


def solution(mesh):
    placed = (
        P(("sub", "dev"), None),
        P(("sub", "dev"), None),
        P(("sub", "dev"), None),
        P(("sub", "dev"), None),
        P("dev", None),
        P(("sub", "dev"), None, None),
        P(("sub", "dev"), None),
        P(),
    )
    return jax.shard_map(
        shards,
        mesh=mesh,
        in_specs=placed,
        out_specs=(P(("sub", "dev"), None), P(("sub", "dev"), None)),
        check_vma=False,
    )
```

```python
import jax
import jax.numpy as jnp
import numpy as np
from jax import lax
from jax.experimental import pallas as pl
from jax.experimental.pallas import tpu as pltpu
from jax.sharding import PartitionSpec as P

F32, BF16 = jnp.float32, jnp.bfloat16
EXACT = lax.Precision.HIGHEST
NI, NRHS, NCL, CAP, NC = 1024, 256, 16, 256, 1024
N_SUB, N_DEV, N_X, N_Z = 8, 32, 4, 8
PEERS = N_SUB * N_X
MIB = 1 << 20
LONG = 20 << 30
NN = (((1,), (0,)), ((), ()))
NT = (((1,), (1,)), ((), ()))


def mm(a, b, dims=NN, precision=None):
    return lax.dot_general(a, b, dims, precision=precision, preferred_element_type=F32)


def pieces(v, count):
    out = []
    for i in range(count):
        part = v.astype(BF16)
        out.append(part)
        if i + 1 < count:
            v = v - part.astype(F32)
    return out


def shape(*dims, dtype=F32):
    return jax.ShapeDtypeStruct(dims, dtype)


class Operand:
    def __init__(self, source, target, arrived):
        self.target, self.waited = target, False
        self.copy = pltpu.make_async_copy(source, target, arrived)
        self.copy.start()

    def __call__(self):
        if not self.waited:
            self.copy.wait()
            self.waited = True
        return self.target


class Result:
    def __init__(self, source, target, arrived):
        self.ref, self.target, self.arrived, self.sent = source, target, arrived, 0
        self.copy = pltpu.make_async_copy(source, target, arrived)

    def send(self):
        if not self.sent:
            self.copy.start()
            self.sent = self.ref.shape[0]

    def send_rows(self, count):
        at = pl.ds(self.sent, count)
        pltpu.make_async_copy(self.ref.at[at], self.target.at[at], self.arrived).start()
        self.sent += count


def run(body, outs, ins, smem=(), near=(), near_outs=(), part=None, scratch=(), limit=61, flops=0):
    part = part or {}
    places = {i: pltpu.SMEM for i in smem} | {i: pltpu.VMEM for i in near}
    far = [i for i in range(len(ins)) if i not in places]
    far_outs = [i for i in range(len(outs)) if i not in near_outs]
    rows = {i: part.get(i, (0, ins[i].shape[0])) for i in far}
    buffers = [pltpu.VMEM((rows[i][1],) + ins[i].shape[1:], ins[i].dtype) for i in far]
    buffers += [pltpu.VMEM(outs[i].shape, outs[i].dtype) for i in far_outs]
    count = len(buffers)
    size = sum(int(np.prod(a.shape)) * a.dtype.itemsize for a in list(ins) + list(outs))

    def kernel(*refs):
        given, refs = list(refs[: len(ins)]), refs[len(ins) :]
        made, refs = list(refs[: len(outs)]), refs[len(outs) :]
        held, arrived, rest = refs[:count], refs[count], refs[count + 1 :]
        for n, i in enumerate(far):
            begin, length = rows[i]
            source = given[i] if length == ins[i].shape[0] else given[i].at[pl.ds(begin, length)]
            given[i] = Operand(source, held[n], arrived.at[n])
        for n, i in enumerate(far_outs, len(far)):
            made[i] = Result(held[n], made[i], arrived.at[n])
        body(given, made, *rest)
        for i in far_outs:
            made[i].send()
        for i in far:
            given[i]()
        for i in far_outs:
            made[i].copy.wait()

    return pl.pallas_call(
        kernel,
        out_shape=list(outs),
        in_specs=[pl.BlockSpec(memory_space=places.get(i, pltpu.HBM)) for i in range(len(ins))],
        out_specs=[
            pl.BlockSpec(memory_space=pltpu.VMEM if i in near_outs else pltpu.HBM)
            for i in range(len(outs))
        ],
        scratch_shapes=buffers + [pltpu.SemaphoreType.DMA((max(count, 1),))] + list(scratch),
        compiler_params=pltpu.CompilerParams(vmem_limit_bytes=int(limit * MIB)),
        cost_estimate=pl.CostEstimate(flops=flops, bytes_accessed=size, transcendentals=0),
        name=body.__name__,
    )(*ins)


def slot_weights(me, stiffness):
    p = me[0] * N_DEV + me[1]
    lanes = iota((1, NRHS), 1)

    def value(q):
        q = jnp.clip(q, 0, N_SUB * N_DEV - 1)
        one = jnp.sum(jnp.where(lanes == q, stiffness, 0.0), axis=1, keepdims=True)
        return jnp.broadcast_to(one, (1, NRHS))

    own = value(p)
    return [own / (own + value(p + shift)) for shift in (-N_DEV, N_DEV, -1, 1)]


def iota(dims, axis):
    return lax.broadcasted_iota(jnp.int32, dims, axis)


def slot_major(dof):
    wide = jnp.concatenate([dof.astype(F32), jnp.zeros((4, CAP), F32)], axis=0)
    columns = jnp.transpose(wide)
    lanes = iota((CAP, NI), 1).astype(F32)
    return [jnp.where(columns[:, k : k + 1] == lanes, 1.0, 0.0).astype(BF16) for k in range(4)]


def unknown_major(dof):
    rows = iota((NI, CAP), 0)
    return [jnp.where(rows == dof[k : k + 1, :], 1.0, 0.0).astype(BF16) for k in range(4)]


def rows_of(k):
    return slice(k * CAP, (k + 1) * CAP)


HROWS = CAP + NCL + 8


def prepare(given, made, perm, wide):
    me, dof, names, stiffness, basis, load = given
    *hs, weights_out = made
    for k, block in enumerate(slot_major(dof()[...])):
        perm[rows_of(k), :] = block
    tiled = jnp.where(
        lax.rem(iota((NCL, NRHS), 1), NCL) == iota((NCL, NRHS), 0), 1.0, 0.0
    ).astype(BF16)
    ids = pieces(jnp.broadcast_to(names()[...].astype(F32), (8, NCL)), 2)
    ids = mm(ids[0], tiled) + mm(ids[1], tiled)
    weights = slot_weights(me, stiffness()[...])
    basis_parts = jnp.concatenate(pieces(basis()[...], 3), axis=0)
    for k, h in enumerate(hs):
        weights_out.ref[k : k + 1, :] = weights[k]
        three = mm(basis_parts, perm[rows_of(k), :], NT)
        h[CAP : CAP + NCL, :] = weights[k] * (
            three[:NCL] + three[NCL : 2 * NCL] + three[2 * NCL :]
        )
        h[CAP + NCL :, :] = ids
    weights_out.ref[4:8, :] = jnp.zeros((4, NRHS), F32)
    weights_out.send()
    for i, part in enumerate(pieces(load()[...], 3)):
        wide[:, i * NRHS : (i + 1) * NRHS] = part
    for k, h in enumerate(hs):
        both = mm(perm[rows_of(k), :], wide[...])
        h[0:CAP, :] = both[:, :NRHS] + both[:, NRHS : 2 * NRHS] + both[:, 2 * NRHS :]


def order(dof, source, target, perm, half):
    for k, block in enumerate(slot_major(dof)):
        perm[rows_of(k), :] = block
    for k in range(4):
        half[rows_of(k), :] = mm(perm[rows_of(k), :], source()[...]).astype(BF16)
    for k in range(4):
        target.ref[rows_of(k), :] = mm(half[rows_of(k), :], perm[...], NT).astype(BF16)
        target.send_rows(CAP)


def order_inverse(given, made, perm, half):
    dof, inverse = given
    order(dof()[...], inverse, made[0], perm, half)


def order_schur(given, made, perm, half):
    dof, schur = given
    order(dof()[...], schur, made[0], perm, half)


def plane_rows(given, made):
    me, blocks = given[0], given[1:]
    x = lax.rem(me[1], N_X)
    for i, block in enumerate(blocks):
        at = lax.rem(x + (N_X - i), N_X) * 32
        made[0][pl.ds(pl.multiple_of(at, 32), 32), :] = block[...]


def block_product(matrix, wide):
    both = mm(matrix[...], wide[...])
    both = both[:, :NRHS] + both[:, NRHS:]
    return [both[rows_of(k), :] for k in range(4)]


def split_into(wide, k, v):
    for i, part in enumerate(pieces(v, 2)):
        wide[rows_of(k), i * NRHS : (i + 1) * NRHS] = part


def project(rows, k, v):
    four = mm(rows[:, rows_of(k)], jnp.concatenate(pieces(v, 2), axis=1))
    return four[:128, :NRHS] + four[:128, NRHS:] + four[128:, :NRHS]


def solved_pieces(solved):
    high, low = pieces(solved[...], 2)
    return jnp.concatenate([high, high, low], axis=1)


def lane_slot(j):
    return lax.div(iota((8, 128), 1), NCL) == j


def place_basis(me, hs, gs, placed):
    s, d = me[0], me[1]
    x = lax.rem(d, N_X)
    odd = lax.rem(s, 2)
    own = odd * 4 + x
    across, over, edge = (
        (1 - odd) * 4 + x,
        (1 - odd) * 4 + lax.rem(x + 1, 4),
        (1 - odd) * 4 + lax.rem(x + 2, 4),
    )
    places = (
        jnp.where(odd == 1, across, over),
        jnp.where(odd == 1, over, across),
        jnp.where(x > 0, odd * 4 + x - 1, edge),
        jnp.where(x < N_X - 1, odd * 4 + x + 1, edge),
    )
    placed[...] = jnp.zeros_like(placed)
    for k in range(4):
        for at, source in ((own, hs[k]), (places[k], gs[k])):
            at = pl.ds(pl.multiple_of(at * NCL, NCL), NCL)
            placed[at, rows_of(k)] = source[CAP : CAP + NCL, :]
    return s, x, own


def fill_rows(rows, placed):
    for i, part in enumerate(pieces(placed[...], 2)):
        rows[i * 128 : (i + 1) * 128, :] = part


def lane_sum(v):
    return jnp.sum(jnp.transpose(v), axis=0, keepdims=True)


def rows_out(out, rows):
    full = 8 - sum(row.shape[0] for row in rows)
    out.ref[...] = jnp.concatenate(list(rows) + [jnp.zeros((full, NRHS), F32)], axis=0)


def begin(given, made, rows):
    me, hs, gs = given[0], given[1:5], given[5:9]
    send, sent, r_out, placed = made
    s, x, own = place_basis(me, hs, gs, placed.ref)
    placed.send()
    for k in range(4):
        r_out.ref[rows_of(k), :] = hs[k][0:CAP, :] + gs[k][0:CAP, :]
        r_out.send_rows(CAP)
    fill_rows(rows, placed.ref)
    total = jnp.zeros((128, NRHS), F32)
    for k in range(4):
        total = total + project(rows, k, hs[k][0:CAP, :])
    flipped = jnp.transpose(total)
    sent.ref[...] = flipped
    sent.send()
    zero = jnp.zeros((8, 128), F32)
    line = iota((8, 128), 0)
    mine = jnp.where(lane_slot(own), hs[0][CAP + NCL :, 0:128], zero)
    before = jnp.where(lane_slot(s) & (x == 0), gs[2][CAP + NCL :, 0:128], zero)
    after = jnp.where(lane_slot(s) & (x == N_X - 1), gs[3][CAP + NCL :, 0:128], zero)
    extra = jnp.where(line == 0, mine, jnp.where(line == 1, before, jnp.where(line == 2, after, zero)))
    for m in range(PEERS):
        send[m * 16 : m * 16 + 8, :] = flipped[m * 8 : m * 8 + 8, :]
        send[m * 16 + 8 : m * 16 + 16, :] = extra


def begin_local(given, made, wide):
    weights, r, inverse = given
    energy, *es = made
    weights = weights()
    for k in range(4):
        split_into(wide, k, weights[k : k + 1, :] * r()[rows_of(k), :])
    total = jnp.zeros((1, NRHS), F32)
    for k, (e, value) in enumerate(zip(es, block_product(inverse(), wide))):
        value = weights[k : k + 1, :] * value
        e.ref[...] = value
        e.send()
        total = total + jnp.sum(value * r()[rows_of(k), :], axis=0, keepdims=True)
    rows_out(energy, [total])


def three_wide(out, v):
    high, low = pieces(v, 2)
    out[:, 0:128] = high
    out[:, 128:256] = low
    out[:, 256:384] = high


def basis_tables(given, made):
    placed, schur = given
    rows, columns, images, coarse = made
    fill_rows(rows.ref, placed())
    rows.send()
    three_wide(columns.ref, jnp.transpose(placed()[...]))
    columns.send()
    both = mm(schur()[...], columns.ref[:, 0:256])
    three_wide(images.ref, both[:, :128] + both[:, 128:])
    images.send()
    four = mm(rows.ref[...], images.ref[:, 0:256])
    coarse.ref[...] = four[:128, :128] + four[:128, 128:] + four[128:, :128]


def layout(m):
    s, x = divmod(m, N_X)
    odd = s % 2
    keep = [odd * 4 + x, (1 - odd) * 4 + x]
    keep += [odd * 4 + v for v in (x - 1, x + 1) if 0 <= v < N_X]
    moves = []
    other = s + 1 if odd else s - 1
    if 0 <= other < N_SUB:
        moves.append(((1 - odd) * 4 + (x + 1) % 4, other // 2, (1 - odd) * 4 + x))
    if x in (0, N_X - 1):
        moves.append(((1 - odd) * 4 + (x + 2) % 4, 4 if x == 0 else 5, s))
    return s // 2, keep, moves


def lanes_in(slots):
    at = lax.div(iota((8, 128), 1), NCL)
    hit = at == slots[0]
    for j in slots[1:]:
        hit = hit | (at == j)
    return hit


def roll_slots(v, shift):
    shift = (shift * NCL) % 128
    return pltpu.roll(v, shift, 1) if shift else v


def spread(tiles):
    groups = [jnp.zeros((8, 128), F32) for _ in range(6)]
    for m in range(PEERS):
        base, keep, moves = layout(m)
        tile = tiles(m)
        groups[base] = groups[base] + jnp.where(lanes_in(keep), tile, 0.0)
        for here, group, there in moves:
            part = roll_slots(jnp.where(lanes_in([here]), tile, 0.0), there - here)
            groups[group] = groups[group] + part
    return jnp.concatenate(groups, axis=1)


def fold(groups, pick, out):
    three = mm(jnp.concatenate(pieces(groups, 3), axis=0), pick, NT)
    result = three[0:8] + three[8:16] + three[16:24]
    for z in range(N_Z):
        out[z * 8 : z * 8 + 8, :] = result


def gather_first(given, made):
    received = given[0]
    out, pick_out = made
    groups = spread(lambda m: received[m * 16 : m * 16 + 8, :])
    ids = [jnp.zeros((8, 128), F32) for _ in range(6)]
    for m in range(PEERS):
        extra = received[m * 16 + 8 : m * 16 + 16, :]
        base = m // 8
        ids[base] = ids[base] + extra
        ids[4] = ids[4] + extra
        ids[5] = ids[5] + extra
    index = jnp.concatenate(
        [ids[0][0:1], ids[1][0:1], ids[2][0:1], ids[3][0:1], ids[4][1:2], ids[5][2:3]], axis=1
    ).astype(jnp.int32)
    pick = jnp.where(iota((NC, 768), 0) == index, 1.0, 0.0).astype(BF16)
    pick_out[...] = pick
    fold(groups, pick, out)


def gather_again(given, made):
    received, pick = given
    groups = spread(lambda m: received[m * 8 : m * 8 + 8, :])
    fold(groups, pick[...], made[0])


def coarse_solve(given, made):
    received, plane = given
    out = made[0]
    rhs = received[0:8, :]
    for z in range(1, N_Z):
        rhs = rhs + received[z * 8 : z * 8 + 8, :]
    solved = mm(rhs, plane[...], NT, precision=EXACT)
    for z in range(N_Z):
        out[z * 8 : z * 8 + 8, :] = solved


def give_back(given, made):
    received, pick = given
    out = made[0]
    solved = jnp.concatenate([received[z * 8 : z * 8 + 8, :] for z in range(N_Z)], axis=1)
    three = mm(jnp.concatenate(pieces(solved, 3), axis=0), pick[...])
    every = three[0:8] + three[8:16] + three[16:24]
    groups = [every[:, g * 128 : (g + 1) * 128] for g in range(6)]
    for m in range(PEERS):
        base, keep, moves = layout(m)
        tile = jnp.where(lanes_in(keep), groups[base], 0.0)
        for here, group, there in moves:
            tile = jnp.where(lanes_in([here]), roll_slots(groups[group], here - there), tile)
        out[m * 8 : m * 8 + 8, :] = tile


def middle(schur, rows, halves, local_out, image, send_local, wide):
    for k in range(4):
        local = halves[k]()[...] + halves[k + 4]()[...]
        local_out.ref[rows_of(k), :] = local
        local_out.send_rows(CAP)
        split_into(wide, k, local)
    total = jnp.zeros((128, NRHS), F32)
    energy = jnp.zeros((1, NRHS), F32)
    for k, value in enumerate(block_product(schur(), wide)):
        image.ref[rows_of(k), :] = value
        image.send_rows(CAP)
        energy = energy + jnp.sum(value * local_out.ref[rows_of(k), :], axis=0, keepdims=True)
        total = total + project(rows(), k, value)
    send_local.ref[...] = jnp.transpose(total)
    send_local.send()
    return energy


def first_middle(given, made, wide):
    schur, rows, *halves = given
    local_out, image, send_local, energy = made
    rows_out(energy, [middle(schur, rows, halves, local_out, image, send_local, wide)])


def energies(solved, sent, send_local, coarse):
    cross = 2.0 * send_local + mm(solved, coarse, NT, precision=EXACT)
    return lane_sum(solved * sent), lane_sum(solved * cross)


def first_send(given, made):
    solved, send_local, coarse = given
    product = mm(solved[...], coarse[...], NT, precision=EXACT)
    made[0][...] = send_local[...] + product


def add_coarse(given, made):
    solved, columns, images, local, image = given
    vector, *outs = made
    back = solved_pieces(solved)
    for k, out in enumerate(outs):
        rows = rows_of(k)
        out.ref[...] = image()[rows, :] + mm(images()[rows, :], back, NT)
        out.send()
    for k in range(4):
        rows = rows_of(k)
        vector.ref[rows, :] = local()[rows, :] + mm(columns()[rows, :], back, NT)
        vector.send_rows(CAP)


def first_direction(given, made):
    add_coarse(given, made)


def second_direction(given, made):
    add_coarse(given, made)


def second_local(given, made, wide):
    weights, *halves = given[:9]
    inverse, energy, other, solved, sent, send_local, coarse = given[9:]
    t_out, dots, *es = made
    weights = weights()
    for k in range(4):
        t = halves[k]()[...] + halves[k + 4]()[...]
        t_out.ref[rows_of(k), :] = t
        t_out.send_rows(CAP)
        split_into(wide, k, weights[k : k + 1, :] * t)
    total = jnp.zeros((1, NRHS), F32)
    for k, (e, value) in enumerate(zip(es, block_product(inverse(), wide))):
        value = weights[k : k + 1, :] * value
        e.ref[...] = value
        e.send()
        total = total + jnp.sum(value * t_out.ref[rows_of(k), :], axis=0, keepdims=True)
    norm, curvature = energies(solved()[...], sent()[...], send_local()[...], coarse()[...])
    rows_out(dots, [energy()[0:1, :] + norm, other()[0:1, :] + curvature, total])


def second_middle(given, made, wide):
    schur, rows, dots, *halves = given
    local_out, image, send_local, dots_out = made
    energy = middle(schur, rows, halves, local_out, image, send_local, wide)
    rows_out(dots_out, [dots()[0:3, :], energy])


def dots_send(given, made):
    solved, sent, send_local, coarse, dots = given
    first, second = energies(solved[...], sent[...], send_local[...], coarse[...])
    values = (dots[0:1, :], dots[1:2, :], dots[2:3, :] + first, dots[3:4, :] + second)
    tile = jnp.concatenate([v[:, :128] for v in values] + [v[:, 128:] for v in values], axis=0)
    for m in range(PEERS):
        made[0][m * 8 : m * 8 + 8, :] = tile


def add_plane(given, made):
    received, out = given[0], made[0]
    total = received[0:8, :]
    for m in range(1, PEERS):
        total = total + received[m * 8 : m * 8 + 8, :]
    for z in range(N_Z):
        out[z * 8 : z * 8 + 8, :] = total


def finish(given, made, wide, perm_t):
    received, dof, p, v, r, t, *halves = given
    for k, block in enumerate(unknown_major(dof()[...])):
        perm_t[:, rows_of(k)] = block
    total = received[0:8, :]
    for z in range(1, N_Z):
        total = total + received[z * 8 : z * 8 + 8, :]
    norm, curvature, g, h = (
        jnp.concatenate([total[i : i + 1], total[i + 4 : i + 5]], axis=1) for i in range(4)
    )
    step = norm / curvature
    scaled = step * g
    grown = scaled / curvature
    next_norm = (grown - 1.0) * norm
    next_curvature = step * (step * h) - grown * scaled
    next_step = next_norm / next_curvature
    both = step + next_step * grown
    cross = next_step * step
    for k in range(4):
        rows = rows_of(k)
        split_into(wide.at[:, 0 : 2 * NRHS], k, both * p()[rows, :] - cross * v()[rows, :])
    for k in range(4):
        rows = rows_of(k)
        w = halves[k]()[...] + halves[k + 4]()[...]
        split_into(
            wide.at[:, 2 * NRHS : 4 * NRHS], k, r()[rows, :] - both * t()[rows, :] + cross * w
        )
    for j, out in enumerate(made):
        two = mm(perm_t[...], wide[:, 2 * j * NRHS : 2 * (j + 1) * NRHS])
        for k in range(4):
            out.ref[rows_of(k), :] = two[rows_of(k), :NRHS] + two[rows_of(k), NRHS:]
            out.send_rows(CAP)


PLANES = [[s * N_DEV + z * N_X + x for s in range(N_SUB) for x in range(N_X)] for z in range(N_Z)]
LINES = [[z * N_X + x for z in range(N_Z)] for x in range(N_X)]


def over_plane(v):
    return lax.all_to_all(v, ("sub", "dev"), 0, 0, tiled=True, axis_index_groups=PLANES)


def over_line(v):
    return lax.all_to_all(v, "dev", 0, 0, tiled=True, axis_index_groups=LINES)


def ring(v, axis, count, shift):
    return lax.ppermute(v, axis, [(i, (i + shift) % count) for i in range(count)])


def halo(blocks):
    return [
        ring(blocks[1], "sub", N_SUB, 1),
        ring(blocks[0], "sub", N_SUB, -1),
        ring(blocks[3], "dev", N_DEV, 1),
        ring(blocks[2], "dev", N_DEV, -1),
    ]


def together(first, *others):
    return lax.optimization_barrier((first, *others))


def small(body, outs, ins, smem=(), flops=LONG):
    return run(
        body,
        outs,
        ins,
        smem=smem,
        near=[i for i in range(len(ins)) if i not in smem],
        near_outs=range(len(outs)),
        limit=12,
        flops=flops,
    )


def shards(
    load, schur, local_inverse, coarse_basis, coarse_inverse, dof_lists, coarse_map, stiffness
):
    me = jnp.stack([lax.axis_index("sub"), lax.axis_index("dev")]).astype(jnp.int32)
    dof = dof_lists[0]
    block = shape(CAP, NRHS)
    vector = shape(NI, NRHS)
    square = shape(NI, NI, dtype=BF16)
    lanes = shape(NRHS, 128)
    table = shape(NI, 384, dtype=BF16)
    wide = pltpu.VMEM((NI, 2 * NRHS), BF16)
    half = pltpu.VMEM((NI, NI), BF16)
    big = 2 * NI * NI * NRHS

    *hs, weights = run(
        prepare,
        [shape(HROWS, NRHS)] * 4 + [shape(8, NRHS)],
        [me, dof, coarse_map, stiffness.reshape(1, -1), coarse_basis, load],
        smem=(0,),
        near_outs=range(4),
        scratch=[half, pltpu.VMEM((NI, 3 * NRHS), BF16)],
        flops=3 * big,
    )
    gs = halo(hs)
    (schur_s,) = run(order_schur, [square], [dof, schur], scratch=[half, half], flops=8 * big)
    coarse_inverse, schur_s = together(coarse_inverse, schur_s)
    planes = [
        lax.ppermute(
            coarse_inverse,
            "dev",
            [(z * N_X + x, z * N_X + (x + i) % N_X) for z in range(N_Z) for x in range(N_X)],
        )
        for i in range(1, N_X)
    ]
    schur_s, *gs = together(schur_s, *gs)
    send, sent, r, placed = run(
        begin,
        [shape(PEERS * 16, 128), lanes, vector, shape(128, NI)],
        [me, *hs, *gs],
        smem=(0,),
        near=range(1, 9),
        near_outs=(0,),
        limit=60.6,
        scratch=[pltpu.VMEM((256, NI), BF16)],
        flops=big // 2,
    )
    (inverse_s,) = run(
        order_inverse, [square], [dof, local_inverse], scratch=[half, half], flops=8 * big
    )
    (plane,) = small(plane_rows, [shape(128, NC)], [me, coarse_inverse, *planes], smem=(0,), flops=0)
    received, inverse_s, plane = together(over_plane(send), inverse_s, plane)
    line, pick = small(gather_first, [shape(N_Z * 8, NC), shape(NC, 768, dtype=BF16)], [received])

    def coarse_middle(received):
        (part,) = small(coarse_solve, [shape(N_Z * 8, 128)], [received, plane])
        return part

    def coarse_end(part):
        (back,) = small(give_back, [shape(PEERS * 8, 128)], [part, pick])
        return back

    energy, *es = run(
        begin_local,
        [shape(8, NRHS)] + [block] * 4,
        [weights, r, inverse_s],
        scratch=[wide],
        flops=2 * big,
    )
    es_halo = halo(es)
    received, energy = together(over_line(line), energy)
    part = coarse_middle(received)
    placed, *es_halo = together(placed, *es_halo)
    rows, columns, images, coarse = run(
        basis_tables,
        [shape(256, NI, dtype=BF16), table, table, shape(128, 128)],
        [placed, schur_s],
        flops=big,
    )
    received, rows, columns, images, coarse = together(
        over_line(part), rows, columns, images, coarse
    )
    back = coarse_end(received)
    local, image, send_local, other = run(
        first_middle,
        [vector, vector, lanes, shape(8, NRHS)],
        [schur_s, rows, *es, *es_halo],
        scratch=[wide],
        flops=2 * big,
    )
    solved = over_plane(back)
    (sending,) = small(first_send, [lanes], [solved, send_local, coarse])
    solved, send = together(solved, sending)
    p, *qs = run(
        first_direction,
        [vector] + [block] * 4,
        [solved, columns, images, local, image],
        near=(0,),
        flops=big,
    )
    qs_halo = halo(qs)
    received, *qs = together(over_plane(send), *qs)
    (line,) = small(gather_again, [shape(N_Z * 8, NC)], [received, pick])
    part = coarse_middle(over_line(line))
    _, *qs_halo = together(part, *qs_halo)
    t, dots, *es = run(
        second_local,
        [vector, shape(8, NRHS)] + [block] * 4,
        [weights, *qs, *qs_halo, inverse_s, energy, other, solved, sent, send_local, coarse],
        scratch=[wide],
        flops=2 * big,
    )
    es_halo = halo(es)
    received, dots = together(over_line(part), dots)
    back = coarse_end(received)
    local, image, send_local, dots = run(
        second_middle,
        [vector, vector, lanes, shape(8, NRHS)],
        [schur_s, rows, dots, *es, *es_halo],
        scratch=[wide],
        flops=2 * big,
    )
    solved = over_plane(back)
    (send,) = small(dots_send, [lanes], [solved, sending, send_local, coarse, dots])
    solved, send = together(solved, send)
    v, *us = run(
        second_direction,
        [vector] + [block] * 4,
        [solved, columns, images, local, image],
        near=(0,),
        flops=big,
    )
    us_halo = halo(us)
    received, *us = together(over_plane(send), *us)
    (line,) = small(add_plane, [shape(N_Z * 8, 128)], [received])
    return tuple(
        run(
            finish,
            [vector, vector],
            [over_line(line), dof, p, v, r, t, *us, *us_halo],
            near=(0,),
            scratch=[pltpu.VMEM((NI, 4 * NRHS), BF16), half],
            flops=4 * big,
        )
    )


def solution(mesh):
    placed = (
        P(("sub", "dev"), None),
        P(("sub", "dev"), None),
        P(("sub", "dev"), None),
        P(("sub", "dev"), None),
        P("dev", None),
        P(("sub", "dev"), None, None),
        P(("sub", "dev"), None),
        P(),
    )
    return jax.shard_map(
        shards,
        mesh=mesh,
        in_specs=placed,
        out_specs=(P(("sub", "dev"), None), P(("sub", "dev"), None)),
        check_vma=False,
    )
```

```python
import jax
import jax.numpy as jnp
import numpy as np
from jax import lax
from jax.experimental import pallas as pl
from jax.experimental.pallas import tpu as pltpu
from jax.sharding import PartitionSpec as P

F32, BF16 = jnp.float32, jnp.bfloat16
EXACT = lax.Precision.HIGHEST
NI, NRHS, NCL, CAP, NC = 1024, 256, 16, 256, 1024
N_SUB, N_DEV, N_X, N_Z = 8, 32, 4, 8
PEERS = N_SUB * N_X
MIB = 1 << 20
LONG = 20 << 30
NN = (((1,), (0,)), ((), ()))
NT = (((1,), (1,)), ((), ()))


def mm(a, b, dims=NN, precision=None):
    return lax.dot_general(a, b, dims, precision=precision, preferred_element_type=F32)


def pieces(v, count):
    out = []
    for i in range(count):
        part = v.astype(BF16)
        out.append(part)
        if i + 1 < count:
            v = v - part.astype(F32)
    return out


def shape(*dims, dtype=F32):
    return jax.ShapeDtypeStruct(dims, dtype)


CHUNK = 256 << 10


def start_copies(source, target, arrived, rows, itemsize):
    size = int(np.prod(target.shape[1:])) * itemsize
    step = max(16, CHUNK // size // 16 * 16)
    for first in range(0, rows, step):
        at = pl.ds(first, min(step, rows - first))
        pltpu.make_async_copy(source.at[at], target.at[at], arrived).start()


class Operand:
    def __init__(self, source, target, arrived):
        self.target, self.waited = target, False
        self.copy = pltpu.make_async_copy(source, target, arrived)
        start_copies(source, target, arrived, target.shape[0], target.dtype.itemsize)

    def __call__(self):
        if not self.waited:
            self.copy.wait()
            self.waited = True
        return self.target


class Result:
    def __init__(self, source, target, arrived):
        self.ref, self.target, self.arrived, self.sent = source, target, arrived, 0
        self.copy = pltpu.make_async_copy(source, target, arrived)

    def send(self):
        if not self.sent:
            self.sent = self.ref.shape[0]
            start_copies(self.ref, self.target, self.arrived, self.sent, self.ref.dtype.itemsize)

    def send_rows(self, count):
        at = pl.ds(self.sent, count)
        pltpu.make_async_copy(self.ref.at[at], self.target.at[at], self.arrived).start()
        self.sent += count


def run(body, outs, ins, smem=(), near=(), near_outs=(), part=None, scratch=(), limit=61, flops=0):
    part = part or {}
    places = {i: pltpu.SMEM for i in smem} | {i: pltpu.VMEM for i in near}
    far = [i for i in range(len(ins)) if i not in places]
    far_outs = [i for i in range(len(outs)) if i not in near_outs]
    rows = {i: part.get(i, (0, ins[i].shape[0])) for i in far}
    buffers = [pltpu.VMEM((rows[i][1],) + ins[i].shape[1:], ins[i].dtype) for i in far]
    buffers += [pltpu.VMEM(outs[i].shape, outs[i].dtype) for i in far_outs]
    count = len(buffers)
    size = sum(int(np.prod(a.shape)) * a.dtype.itemsize for a in list(ins) + list(outs))

    def kernel(*refs):
        given, refs = list(refs[: len(ins)]), refs[len(ins) :]
        made, refs = list(refs[: len(outs)]), refs[len(outs) :]
        held, arrived, rest = refs[:count], refs[count], refs[count + 1 :]
        for n, i in enumerate(far):
            begin, length = rows[i]
            source = given[i] if length == ins[i].shape[0] else given[i].at[pl.ds(begin, length)]
            given[i] = Operand(source, held[n], arrived.at[n])
        for n, i in enumerate(far_outs, len(far)):
            made[i] = Result(held[n], made[i], arrived.at[n])
        body(given, made, *rest)
        for i in far_outs:
            made[i].send()
        for i in far:
            given[i]()
        for i in far_outs:
            made[i].copy.wait()

    return pl.pallas_call(
        kernel,
        out_shape=list(outs),
        in_specs=[pl.BlockSpec(memory_space=places.get(i, pltpu.HBM)) for i in range(len(ins))],
        out_specs=[
            pl.BlockSpec(memory_space=pltpu.VMEM if i in near_outs else pltpu.HBM)
            for i in range(len(outs))
        ],
        scratch_shapes=buffers + [pltpu.SemaphoreType.DMA((max(count, 1),))] + list(scratch),
        compiler_params=pltpu.CompilerParams(vmem_limit_bytes=int(limit * MIB)),
        cost_estimate=pl.CostEstimate(flops=flops, bytes_accessed=size, transcendentals=0),
        name=body.__name__,
    )(*ins)


def slot_weights(stiffness):
    p = lax.axis_index("sub") * N_DEV + lax.axis_index("dev")
    lanes = iota((1, NRHS), 1)

    def value(q):
        q = jnp.clip(q, 0, N_SUB * N_DEV - 1)
        one = jnp.sum(jnp.where(lanes == q, stiffness, 0.0), axis=1, keepdims=True)
        return jnp.broadcast_to(one, (1, NRHS))

    own = value(p)
    return [own / (own + value(p + shift)) for shift in (-N_DEV, N_DEV, -1, 1)]


def iota(dims, axis):
    return lax.broadcasted_iota(jnp.int32, dims, axis)


def slot_major(dof):
    wide = jnp.concatenate([dof.astype(F32), jnp.zeros((4, CAP), F32)], axis=0)
    columns = jnp.transpose(wide)
    lanes = iota((CAP, NI), 1).astype(F32)
    return (jnp.where(columns[:, k : k + 1] == lanes, 1.0, 0.0).astype(BF16) for k in range(4))


def unknown_major(dof):
    rows = iota((NI, CAP), 0)
    return [jnp.where(rows == dof[k : k + 1, :], 1.0, 0.0).astype(BF16) for k in range(4)]


def rows_of(k):
    return slice(k * CAP, (k + 1) * CAP)


HROWS = CAP + NCL + 8


def prepare(given, made, wide):
    dof, basis, load, names, stiffness = given
    *hs, weights_out = made
    blocks = slot_major(dof()[...])
    turned = jnp.transpose(jnp.concatenate([basis()[...], jnp.zeros((48, NI), F32)], axis=0))
    high, low = pieces(turned, 2)
    wide[:, 2 * NRHS : 2 * NRHS + 64] = high
    wide[:, 2 * NRHS + 64 :] = low
    for i, part in enumerate(pieces(load()[...], 2)):
        wide[:, i * NRHS : (i + 1) * NRHS] = part
    tiled = jnp.where(
        lax.rem(iota((NCL, NRHS), 1), NCL) == iota((NCL, NRHS), 0), 1.0, 0.0
    ).astype(BF16)
    ids = pieces(jnp.broadcast_to(names()[...].astype(F32), (8, NCL)), 2)
    ids = mm(ids[0], tiled) + mm(ids[1], tiled)
    weights = slot_weights(stiffness()[...])
    weights_out.ref[...] = jnp.concatenate(weights + [jnp.zeros((4, NRHS), F32)], axis=0)
    weights_out.send()
    for k, h in enumerate(hs):
        both = mm(next(blocks), wide[...])
        h[0:CAP, :] = both[:, :NRHS] + both[:, NRHS : 2 * NRHS]
        own = jnp.transpose(both[:, 2 * NRHS :])
        h[CAP : CAP + NCL, :] = weights[k] * (own[0:NCL] + own[64 : 64 + NCL])
        h[CAP + NCL :, :] = ids


def order(given, made, perm, half):
    dof, source = given
    for k, block in enumerate(slot_major(dof()[...])):
        perm[rows_of(k), :] = block
        half[rows_of(k), :] = mm(block, source()[...]).astype(BF16)
    for k in range(4):
        made[0].ref[rows_of(k), :] = mm(half[rows_of(k), :], perm[...], NT).astype(BF16)
        made[0].send_rows(CAP)


def plane_rows(given, made):
    x = lax.rem(lax.axis_index("dev"), N_X)
    for i, block in enumerate(given):
        at = lax.rem(x + (N_X - i), N_X) * 32
        made[0][pl.ds(pl.multiple_of(at, 32), 32), :] = block[...]


def block_product(matrix, wide):
    both = mm(matrix[...], wide[...])
    both = both[:, :NRHS] + both[:, NRHS:]
    return [both[rows_of(k), :] for k in range(4)]


def split_into(wide, k, v):
    for i, part in enumerate(pieces(v, 2)):
        wide[rows_of(k), i * NRHS : (i + 1) * NRHS] = part


def project(rows, k, v):
    four = mm(rows[:, rows_of(k)], jnp.concatenate(pieces(v, 2), axis=1))
    return four[:128, :NRHS] + four[:128, NRHS:] + four[128:, :NRHS]


def solved_pieces(solved):
    high, low = pieces(solved[...], 2)
    return jnp.concatenate([high, high, low], axis=1)


def lane_slot(j):
    return lax.div(iota((8, 128), 1), NCL) == j


def place_basis(hs, gs, placed):
    s = lax.axis_index("sub")
    x = lax.rem(lax.axis_index("dev"), N_X)
    odd = lax.rem(s, 2)
    own = odd * 4 + x
    across, over, edge = (
        (1 - odd) * 4 + x,
        (1 - odd) * 4 + lax.rem(x + 1, 4),
        (1 - odd) * 4 + lax.rem(x + 2, 4),
    )
    places = (
        jnp.where(odd == 1, across, over),
        jnp.where(odd == 1, over, across),
        jnp.where(x > 0, odd * 4 + x - 1, edge),
        jnp.where(x < N_X - 1, odd * 4 + x + 1, edge),
    )
    placed[...] = jnp.zeros_like(placed)
    for k in range(4):
        for at, source in ((own, hs[k]), (places[k], gs[k])):
            at = pl.ds(pl.multiple_of(at * NCL, NCL), NCL)
            placed[at, rows_of(k)] = source[CAP : CAP + NCL, :]
    return s, x, own


def fill_rows(rows, placed):
    for i, part in enumerate(pieces(placed[...], 2)):
        rows[i * 128 : (i + 1) * 128, :] = part


def lane_sum(v):
    return mm(jnp.ones((8, 128), F32), v, NT, precision=EXACT)[0:1]


def rows_out(out, rows):
    full = 8 - sum(row.shape[0] for row in rows)
    out.ref[...] = jnp.concatenate(list(rows) + [jnp.zeros((full, NRHS), F32)], axis=0)


def begin(given, made, rows):
    hs, gs = given[0:4], given[4:8]
    send, sent, r_out, placed = made
    s, x, own = place_basis(hs, gs, placed.ref)
    placed.send()
    for k in range(4):
        r_out.ref[rows_of(k), :] = hs[k][0:CAP, :] + gs[k][0:CAP, :]
        r_out.send_rows(CAP)
    fill_rows(rows, placed.ref)
    total = jnp.zeros((128, NRHS), F32)
    for k in range(4):
        total = total + project(rows, k, hs[k][0:CAP, :])
    flipped = jnp.transpose(total)
    sent.ref[...] = flipped
    sent.send()
    zero = jnp.zeros((8, 128), F32)
    line = iota((8, 128), 0)
    mine = jnp.where(lane_slot(own), hs[0][CAP + NCL :, 0:128], zero)
    before = jnp.where(lane_slot(s) & (x == 0), gs[2][CAP + NCL :, 0:128], zero)
    after = jnp.where(lane_slot(s) & (x == N_X - 1), gs[3][CAP + NCL :, 0:128], zero)
    extra = jnp.where(line == 0, mine, jnp.where(line == 1, before, jnp.where(line == 2, after, zero)))
    for m in range(PEERS):
        send[m * 16 : m * 16 + 8, :] = flipped[m * 8 : m * 8 + 8, :]
        send[m * 16 + 8 : m * 16 + 16, :] = extra


def begin_local(given, made, wide):
    weights, r, inverse = given
    energy, *es = made
    weights = weights()
    for k in range(4):
        split_into(wide, k, weights[k : k + 1, :] * r()[rows_of(k), :])
    total = jnp.zeros((1, NRHS), F32)
    for k, (e, value) in enumerate(zip(es, block_product(inverse(), wide))):
        value = weights[k : k + 1, :] * value
        e.ref[...] = value
        e.send()
        total = total + jnp.sum(value * r()[rows_of(k), :], axis=0, keepdims=True)
    rows_out(energy, [total])


def three_wide(out, v):
    high, low = pieces(v, 2)
    out[:, 0:128] = high
    out[:, 128:256] = low
    out[:, 256:384] = high


def basis_tables(given, made):
    placed, schur = given
    rows, columns, images, coarse = made
    fill_rows(rows.ref, placed())
    rows.send()
    three_wide(columns.ref, jnp.transpose(placed()[...]))
    columns.send()
    both = mm(schur()[...], columns.ref[:, 0:256])
    three_wide(images.ref, both[:, :128] + both[:, 128:])
    images.send()
    four = mm(rows.ref[...], images.ref[:, 0:256])
    coarse.ref[...] = four[:128, :128] + four[:128, 128:] + four[128:, :128]


def layout(m):
    s, x = divmod(m, N_X)
    odd = s % 2
    keep = [odd * 4 + x, (1 - odd) * 4 + x]
    keep += [odd * 4 + v for v in (x - 1, x + 1) if 0 <= v < N_X]
    moves = []
    other = s + 1 if odd else s - 1
    if 0 <= other < N_SUB:
        moves.append(((1 - odd) * 4 + (x + 1) % 4, other // 2, (1 - odd) * 4 + x))
    if x in (0, N_X - 1):
        moves.append(((1 - odd) * 4 + (x + 2) % 4, 4 if x == 0 else 5, s))
    return s // 2, keep, moves


def lanes_in(slots):
    at = lax.div(iota((8, 128), 1), NCL)
    hit = at == slots[0]
    for j in slots[1:]:
        hit = hit | (at == j)
    return hit


def roll_slots(v, shift):
    shift = (shift * NCL) % 128
    return pltpu.roll(v, shift, 1) if shift else v


def spread(tiles):
    groups = [jnp.zeros((8, 128), F32) for _ in range(6)]
    for m in range(PEERS):
        base, keep, moves = layout(m)
        tile = tiles(m)
        groups[base] = groups[base] + jnp.where(lanes_in(keep), tile, 0.0)
        for here, group, there in moves:
            part = roll_slots(jnp.where(lanes_in([here]), tile, 0.0), there - here)
            groups[group] = groups[group] + part
    return jnp.concatenate(groups, axis=1)


def fold(groups, pick, out):
    three = mm(jnp.concatenate(pieces(groups, 3), axis=0), pick, NT)
    result = three[0:8] + three[8:16] + three[16:24]
    for z in range(N_Z):
        out[z * 8 : z * 8 + 8, :] = result


def gather_first(given, made):
    received = given[0]
    out, pick_out = made
    groups = spread(lambda m: received[m * 16 : m * 16 + 8, :])
    ids = [jnp.zeros((8, 128), F32) for _ in range(6)]
    for m in range(PEERS):
        extra = received[m * 16 + 8 : m * 16 + 16, :]
        base = m // 8
        ids[base] = ids[base] + extra
        ids[4] = ids[4] + extra
        ids[5] = ids[5] + extra
    index = jnp.concatenate(
        [ids[0][0:1], ids[1][0:1], ids[2][0:1], ids[3][0:1], ids[4][1:2], ids[5][2:3]], axis=1
    ).astype(jnp.int32)
    pick = jnp.where(iota((NC, 768), 0) == index, 1.0, 0.0).astype(BF16)
    pick_out[...] = pick
    fold(groups, pick, out)


def gather_again(given, made):
    received, pick = given
    groups = spread(lambda m: received[m * 8 : m * 8 + 8, :])
    fold(groups, pick[...], made[0])


def coarse_solve(given, made):
    received, plane = given
    out = made[0]
    rhs = received[0:8, :]
    for z in range(1, N_Z):
        rhs = rhs + received[z * 8 : z * 8 + 8, :]
    solved = mm(rhs, plane[...], NT, precision=EXACT)
    for z in range(N_Z):
        out[z * 8 : z * 8 + 8, :] = solved


def give_back(given, made):
    received, pick = given
    out = made[0]
    solved = jnp.concatenate([received[z * 8 : z * 8 + 8, :] for z in range(N_Z)], axis=1)
    three = mm(jnp.concatenate(pieces(solved, 3), axis=0), pick[...])
    every = three[0:8] + three[8:16] + three[16:24]
    groups = [every[:, g * 128 : (g + 1) * 128] for g in range(6)]
    for m in range(PEERS):
        base, keep, moves = layout(m)
        tile = jnp.where(lanes_in(keep), groups[base], 0.0)
        for here, group, there in moves:
            tile = jnp.where(lanes_in([here]), roll_slots(groups[group], here - there), tile)
        out[m * 8 : m * 8 + 8, :] = tile


def middle(schur, rows, halves, local_out, image, send_local, wide):
    for k in range(4):
        local = halves[k]()[...] + halves[k + 4]()[...]
        local_out.ref[rows_of(k), :] = local
        local_out.send_rows(CAP)
        split_into(wide, k, local)
    total = jnp.zeros((128, NRHS), F32)
    energy = jnp.zeros((1, NRHS), F32)
    for k, value in enumerate(block_product(schur(), wide)):
        image.ref[rows_of(k), :] = value
        image.send_rows(CAP)
        energy = energy + jnp.sum(value * local_out.ref[rows_of(k), :], axis=0, keepdims=True)
        total = total + project(rows(), k, value)
    send_local.ref[0:NRHS, :] = jnp.transpose(total)
    return energy


def first_middle(given, made, wide):
    schur, rows, *halves = given
    local_out, image, send_local, energy = made
    rows_out(energy, [middle(schur, rows, halves, local_out, image, send_local, wide)])


def energies(solved, sent, send_local, coarse):
    cross = 2.0 * send_local + mm(solved, coarse, NT, precision=EXACT)
    return lane_sum(solved * sent), lane_sum(solved * cross)


def first_send(given, made):
    solved, send_local, coarse = given
    product = mm(solved[...], coarse[...], NT, precision=EXACT)
    made[0][...] = send_local[...] + product


def held(v):
    return v() if isinstance(v, Operand) else v


def add_coarse(given, made):
    solved, images, image = given
    kept, *outs = made
    kept.ref[...] = solved[...]
    kept.send()
    back = solved_pieces(solved)
    for k, out in enumerate(outs):
        rows = rows_of(k)
        out.ref[...] = image()[rows, :] + mm(images()[rows, :], back, NT)
        out.send()


def first_direction(given, made):
    add_coarse(given, made)


def second_direction(given, made):
    add_coarse(given, made)


def first_energies(given, made):
    energy, other, solved, sent, send_local, coarse = given
    norm, curvature = energies(solved()[...], sent()[...], send_local()[...], coarse()[...])
    rows_out(made[0], [energy()[0:1, :] + norm, other()[0:1, :] + curvature])


def second_local(given, made, wide):
    weights, *halves = given[:9]
    inverse, dots = given[9:]
    t_out, dots_out, *es = made
    weights = weights()
    for k in range(4):
        t = halves[k]()[...] + halves[k + 4]()[...]
        t_out.ref[rows_of(k), :] = t
        t_out.send_rows(CAP)
        split_into(wide, k, weights[k : k + 1, :] * t)
    total = jnp.zeros((1, NRHS), F32)
    for k, (e, value) in enumerate(zip(es, block_product(inverse(), wide))):
        value = weights[k : k + 1, :] * value
        e.ref[...] = value
        e.send()
        total = total + jnp.sum(value * t_out.ref[rows_of(k), :], axis=0, keepdims=True)
    rows_out(dots_out, [dots()[0:2, :], total])


def second_middle(given, made, wide):
    schur, rows, dots, *halves = given
    local_out, image, packed = made
    energy = middle(schur, rows, halves, local_out, image, packed, wide)
    tail = jnp.concatenate([dots()[0:3, :], energy, jnp.zeros((4, NRHS), F32)], axis=0)
    packed.ref[NRHS : NRHS + 8, :] = tail[:, 0:128]
    packed.ref[NRHS + 8 : NRHS + 16, :] = tail[:, 128:]


def dots_send(given, made):
    solved, sent, packed, coarse = given
    first, second = energies(solved[...], sent[...], packed[0:NRHS, :], coarse[...])
    dots = jnp.concatenate([packed[NRHS : NRHS + 8, :], packed[NRHS + 8 :, :]], axis=1)
    values = (dots[0:1, :], dots[1:2, :], dots[2:3, :] + first, dots[3:4, :] + second)
    tile = jnp.concatenate([v[:, :128] for v in values] + [v[:, 128:] for v in values], axis=0)
    for m in range(PEERS):
        made[0][m * 8 : m * 8 + 8, :] = tile


def add_plane(given, made):
    received, out = given[0], made[0]
    total = received[0:8, :]
    for m in range(1, PEERS):
        total = total + received[m * 8 : m * 8 + 8, :]
    for z in range(N_Z):
        out[z * 8 : z * 8 + 8, :] = total


def vectors(given, made):
    columns, solved, local, solved_too, local_too = given
    for out, back, v in ((made[0], solved, local), (made[1], solved_too, local_too)):
        back = solved_pieces(back())
        for k in range(4):
            rows = rows_of(k)
            out.ref[rows, :] = v()[rows, :] + mm(columns()[rows, :], back, NT)
            out.send_rows(CAP)


def finish(given, made, perm_t, wide):
    received, dof, p, v, r, t, *halves = given
    for k, block in enumerate(unknown_major(dof()[...])):
        perm_t[:, rows_of(k)] = block
    total = received[0:8, :]
    for z in range(1, N_Z):
        total = total + received[z * 8 : z * 8 + 8, :]
    norm, curvature, g, h = (
        jnp.concatenate([total[i : i + 1], total[i + 4 : i + 5]], axis=1) for i in range(4)
    )
    step = norm / curvature
    scaled = step * g
    grown = scaled / curvature
    next_norm = (grown - 1.0) * norm
    next_curvature = step * (step * h) - grown * scaled
    next_step = next_norm / next_curvature
    both = step + next_step * grown
    cross = next_step * step
    for k in range(4):
        rows = rows_of(k)
        split_into(wide.at[:, 0 : 2 * NRHS], k, both * p()[rows, :] - cross * v()[rows, :])
    for k in range(4):
        rows = rows_of(k)
        w = halves[k]()[...] + held(halves[k + 4])[...]
        value = r()[rows, :] - both * t()[rows, :] + cross * w
        split_into(wide.at[:, 2 * NRHS : 4 * NRHS], k, value)
    for j, out in enumerate(made):
        two = mm(perm_t[...], wide[:, 2 * j * NRHS : 2 * (j + 1) * NRHS])
        out.ref[...] = two[:, :NRHS] + two[:, NRHS:]
        out.send()


PLANES = [[s * N_DEV + z * N_X + x for s in range(N_SUB) for x in range(N_X)] for z in range(N_Z)]
LINES = [[z * N_X + x for z in range(N_Z)] for x in range(N_X)]


def over_plane(v):
    return lax.all_to_all(v, ("sub", "dev"), 0, 0, tiled=True, axis_index_groups=PLANES)


def over_line(v):
    return lax.all_to_all(v, "dev", 0, 0, tiled=True, axis_index_groups=LINES)


def ring(v, axis, count, shift):
    return lax.ppermute(v, axis, [(i, (i + shift) % count) for i in range(count)])


def halo(blocks):
    return [
        ring(blocks[1], "sub", N_SUB, 1),
        ring(blocks[0], "sub", N_SUB, -1),
        ring(blocks[3], "dev", N_DEV, 1),
        ring(blocks[2], "dev", N_DEV, -1),
    ]


def together(first, *others):
    return lax.optimization_barrier((first, *others))


def small(body, outs, ins, smem=(), flops=LONG):
    return run(
        body,
        outs,
        ins,
        smem=smem,
        near=[i for i in range(len(ins)) if i not in smem],
        near_outs=range(len(outs)),
        limit=12,
        flops=flops,
    )


def shards(
    load, schur, local_inverse, coarse_basis, coarse_inverse, dof_lists, coarse_map, stiffness
):
    dof = dof_lists[0]
    block = shape(CAP, NRHS)
    vector = shape(NI, NRHS)
    square = shape(NI, NI, dtype=BF16)
    lanes = shape(NRHS, 128)
    table = shape(NI, 384, dtype=BF16)
    wide = pltpu.VMEM((NI, 2 * NRHS), BF16)
    half = pltpu.VMEM((NI, NI), BF16)
    big = 2 * NI * NI * NRHS

    *hs, weights = run(
        prepare,
        [shape(HROWS, NRHS)] * 4 + [shape(8, NRHS)],
        [dof, coarse_basis, load, coarse_map, stiffness.reshape(1, -1)],
        near_outs=range(4),
        scratch=[pltpu.VMEM((NI, 2 * NRHS + 128), BF16)],
        flops=3 * big,
    )
    gs = halo(hs)
    (schur_s,) = run(
        order, [square], [dof, schur], scratch=[half, half], limit=59, flops=8 * big
    )
    coarse_inverse, schur_s = together(coarse_inverse, schur_s)
    planes = [
        lax.ppermute(
            coarse_inverse,
            "dev",
            [(z * N_X + x, z * N_X + (x + i) % N_X) for z in range(N_Z) for x in range(N_X)],
        )
        for i in range(1, N_X)
    ]
    schur_s, *gs = together(schur_s, *gs)
    send, sent, r, placed = run(
        begin,
        [shape(PEERS * 16, 128), lanes, vector, shape(128, NI)],
        [*hs, *gs],
        near=range(8),
        near_outs=(0,),
        limit=60.2,
        scratch=[pltpu.VMEM((256, NI), BF16)],
        flops=big // 2,
    )
    (inverse_s,) = run(order, [square], [dof, local_inverse], scratch=[half, half], flops=8 * big)
    (plane,) = small(plane_rows, [shape(128, NC)], [coarse_inverse, *planes], flops=0)
    received, inverse_s, plane = together(over_plane(send), inverse_s, plane)
    line, pick = small(gather_first, [shape(N_Z * 8, NC), shape(NC, 768, dtype=BF16)], [received])

    def coarse_middle(received):
        (part,) = small(coarse_solve, [shape(N_Z * 8, 128)], [received, plane])
        return part

    def coarse_end(part):
        (back,) = small(give_back, [shape(PEERS * 8, 128)], [part, pick])
        return back

    energy, *es = run(
        begin_local,
        [shape(8, NRHS)] + [block] * 4,
        [weights, r, inverse_s],
        scratch=[wide],
        flops=2 * big,
    )
    es_halo = halo(es)
    received, energy = together(over_line(line), energy)
    part = coarse_middle(received)
    placed, *es_halo = together(placed, *es_halo)
    rows, columns, images, coarse = run(
        basis_tables,
        [shape(256, NI, dtype=BF16), table, table, shape(128, 128)],
        [placed, schur_s],
        flops=big,
    )
    received, rows, columns, images, coarse = together(
        over_line(part), rows, columns, images, coarse
    )
    back = coarse_end(received)
    local, image, send_local, other = run(
        first_middle,
        [vector, vector, lanes, shape(8, NRHS)],
        [schur_s, rows, *es, *es_halo],
        scratch=[wide],
        flops=2 * big,
    )
    solved = over_plane(back)
    (sending,) = small(first_send, [lanes], [solved, send_local, coarse])
    solved, send = together(solved, sending)
    kept, *qs = run(
        first_direction,
        [lanes] + [block] * 4,
        [solved, images, image],
        near=(0,),
        flops=big,
    )
    qs_halo = halo(qs)
    received, *qs = together(over_plane(send), *qs)
    (line,) = small(gather_again, [shape(N_Z * 8, NC)], [received, pick])
    (dots,) = run(
        first_energies, [shape(8, NRHS)], [energy, other, kept, sent, send_local, coarse]
    )
    received, dots = together(over_line(line), dots)
    part = coarse_middle(received)
    _, inverse_s = together(part, inverse_s)
    t, dots, *es = run(
        second_local,
        [vector, shape(8, NRHS)] + [block] * 4,
        [weights, *qs, *qs_halo, inverse_s, dots],
        scratch=[wide],
        flops=2 * big,
    )
    es_halo = halo(es)
    received, dots = together(over_line(part), dots)
    back = coarse_end(received)
    local_too, image, packed = run(
        second_middle,
        [vector, vector, shape(NRHS + 16, 128)],
        [schur_s, rows, dots, *es, *es_halo],
        scratch=[wide],
        flops=2 * big,
    )
    solved = over_plane(back)
    (send,) = small(dots_send, [lanes], [solved, sending, packed, coarse])
    solved, send = together(solved, send)
    kept_too, *us = run(
        second_direction,
        [lanes] + [block] * 4,
        [solved, images, image],
        near=(0,),
        flops=big,
    )
    us_halo = halo(us)
    received, *us = together(over_plane(send), *us)
    (line,) = small(add_plane, [shape(N_Z * 8, 128)], [received])
    line, local_too = together(line, local_too)
    p, v = run(
        vectors,
        [vector, vector],
        [columns, kept, local, kept_too, local_too],
        flops=big // 2,
    )
    received, p, v = together(over_line(line), p, v)
    return tuple(
        run(
            finish,
            [vector, vector],
            [received, dof, p, v, r, t, *us, *us_halo],
            near=(0, 10, 11, 12, 13),
            limit=59,
            scratch=[half, pltpu.VMEM((NI, 4 * NRHS), BF16)],
            flops=4 * big,
        )
    )


def solution(mesh):
    placed = (
        P(("sub", "dev"), None),
        P(("sub", "dev"), None),
        P(("sub", "dev"), None),
        P(("sub", "dev"), None),
        P("dev", None),
        P(("sub", "dev"), None, None),
        P(("sub", "dev"), None),
        P(),
    )
    return jax.shard_map(
        shards,
        mesh=mesh,
        in_specs=placed,
        out_specs=(P(("sub", "dev"), None), P(("sub", "dev"), None)),
        check_vma=False,
    )
```

```python
import jax
import jax.numpy as jnp
import numpy as np
from jax import lax
from jax.experimental import pallas as pl
from jax.experimental.pallas import tpu as pltpu
from jax.sharding import PartitionSpec as P

F32, BF16 = jnp.float32, jnp.bfloat16
EXACT = lax.Precision.HIGHEST
NI, NRHS, NCL, CAP, NC = 1024, 256, 16, 256, 1024
N_SUB, N_DEV, N_X, N_Z = 8, 32, 4, 8
PEERS = N_SUB * N_X
MIB = 1 << 20
LONG = 20 << 30
NN = (((1,), (0,)), ((), ()))
NT = (((1,), (1,)), ((), ()))


def mm(a, b, dims=NN, precision=None):
    return lax.dot_general(a, b, dims, precision=precision, preferred_element_type=F32)


def pieces(v, count):
    out = []
    for i in range(count):
        part = v.astype(BF16)
        out.append(part)
        if i + 1 < count:
            v = v - part.astype(F32)
    return out


def shape(*dims, dtype=F32):
    return jax.ShapeDtypeStruct(dims, dtype)


CHUNK = 256 << 10


def start_copies(source, target, arrived, rows, itemsize):
    size = int(np.prod(target.shape[1:])) * itemsize
    step = max(16, CHUNK // size // 16 * 16)
    for first in range(0, rows, step):
        at = pl.ds(first, min(step, rows - first))
        pltpu.make_async_copy(source.at[at], target.at[at], arrived).start()


class Operand:
    def __init__(self, source, target, arrived):
        self.target, self.waited = target, False
        self.copy = pltpu.make_async_copy(source, target, arrived)
        start_copies(source, target, arrived, target.shape[0], target.dtype.itemsize)

    def __call__(self):
        if not self.waited:
            self.copy.wait()
            self.waited = True
        return self.target


class Result:
    def __init__(self, source, target, arrived):
        self.ref, self.target, self.arrived, self.sent = source, target, arrived, 0
        self.copy = pltpu.make_async_copy(source, target, arrived)

    def send(self):
        if not self.sent:
            self.sent = self.ref.shape[0]
            start_copies(self.ref, self.target, self.arrived, self.sent, self.ref.dtype.itemsize)

    def send_rows(self, count):
        at = pl.ds(self.sent, count)
        pltpu.make_async_copy(self.ref.at[at], self.target.at[at], self.arrived).start()
        self.sent += count


def run(body, outs, ins, smem=(), near=(), near_outs=(), part=None, scratch=(), limit=61, flops=0):
    part = part or {}
    places = {i: pltpu.SMEM for i in smem} | {i: pltpu.VMEM for i in near}
    far = [i for i in range(len(ins)) if i not in places]
    far_outs = [i for i in range(len(outs)) if i not in near_outs]
    rows = {i: part.get(i, (0, ins[i].shape[0])) for i in far}
    buffers = [pltpu.VMEM((rows[i][1],) + ins[i].shape[1:], ins[i].dtype) for i in far]
    buffers += [pltpu.VMEM(outs[i].shape, outs[i].dtype) for i in far_outs]
    count = len(buffers)
    size = sum(int(np.prod(a.shape)) * a.dtype.itemsize for a in list(ins) + list(outs))

    def kernel(*refs):
        given, refs = list(refs[: len(ins)]), refs[len(ins) :]
        made, refs = list(refs[: len(outs)]), refs[len(outs) :]
        held, arrived, rest = refs[:count], refs[count], refs[count + 1 :]
        for n, i in enumerate(far):
            begin, length = rows[i]
            source = given[i] if length == ins[i].shape[0] else given[i].at[pl.ds(begin, length)]
            given[i] = Operand(source, held[n], arrived.at[n])
        for n, i in enumerate(far_outs, len(far)):
            made[i] = Result(held[n], made[i], arrived.at[n])
        body(given, made, *rest)
        for i in far_outs:
            made[i].send()
        for i in far:
            given[i]()
        for i in far_outs:
            made[i].copy.wait()

    return pl.pallas_call(
        kernel,
        out_shape=list(outs),
        in_specs=[pl.BlockSpec(memory_space=places.get(i, pltpu.HBM)) for i in range(len(ins))],
        out_specs=[
            pl.BlockSpec(memory_space=pltpu.VMEM if i in near_outs else pltpu.HBM)
            for i in range(len(outs))
        ],
        scratch_shapes=buffers + [pltpu.SemaphoreType.DMA((max(count, 1),))] + list(scratch),
        compiler_params=pltpu.CompilerParams(vmem_limit_bytes=int(limit * MIB)),
        cost_estimate=pl.CostEstimate(flops=flops, bytes_accessed=size, transcendentals=0),
        name=body.__name__,
    )(*ins)


def slot_weights(stiffness):
    p = lax.axis_index("sub") * N_DEV + lax.axis_index("dev")
    lanes = iota((1, NRHS), 1)

    def value(q):
        q = jnp.clip(q, 0, N_SUB * N_DEV - 1)
        one = jnp.sum(jnp.where(lanes == q, stiffness, 0.0), axis=1, keepdims=True)
        return jnp.broadcast_to(one, (1, NRHS))

    own = value(p)
    return [own / (own + value(p + shift)) for shift in (-N_DEV, N_DEV, -1, 1)]


def iota(dims, axis):
    return lax.broadcasted_iota(jnp.int32, dims, axis)


def slot_major(dof):
    wide = jnp.concatenate([dof.astype(F32), jnp.zeros((4, CAP), F32)], axis=0)
    columns = jnp.transpose(wide)
    lanes = iota((CAP, NI), 1).astype(F32)
    return (jnp.where(columns[:, k : k + 1] == lanes, 1.0, 0.0).astype(BF16) for k in range(4))


def unknown_major(dof):
    rows = iota((NI, CAP), 0)
    return [jnp.where(rows == dof[k : k + 1, :], 1.0, 0.0).astype(BF16) for k in range(4)]


def rows_of(k):
    return slice(k * CAP, (k + 1) * CAP)


HROWS = CAP + NCL + 8


def prepare(given, made, wide):
    dof, basis, load, names, stiffness = given
    *hs, weights_out = made
    blocks = slot_major(dof()[...])
    turned = jnp.transpose(jnp.concatenate([basis()[...], jnp.zeros((48, NI), F32)], axis=0))
    high, low = pieces(turned, 2)
    wide[:, 2 * NRHS : 2 * NRHS + 64] = high
    wide[:, 2 * NRHS + 64 :] = low
    for i, part in enumerate(pieces(load()[...], 2)):
        wide[:, i * NRHS : (i + 1) * NRHS] = part
    tiled = jnp.where(
        lax.rem(iota((NCL, NRHS), 1), NCL) == iota((NCL, NRHS), 0), 1.0, 0.0
    ).astype(BF16)
    ids = pieces(jnp.broadcast_to(names()[...].astype(F32), (8, NCL)), 2)
    ids = mm(ids[0], tiled) + mm(ids[1], tiled)
    weights = slot_weights(stiffness()[...])
    weights_out.ref[...] = jnp.concatenate(weights + [jnp.zeros((4, NRHS), F32)], axis=0)
    weights_out.send()
    for k, h in enumerate(hs):
        both = mm(next(blocks), wide[...])
        h[0:CAP, :] = both[:, :NRHS] + both[:, NRHS : 2 * NRHS]
        own = jnp.transpose(both[:, 2 * NRHS :])
        h[CAP : CAP + NCL, :] = weights[k] * (own[0:NCL] + own[64 : 64 + NCL])
        h[CAP + NCL :, :] = ids


def order(given, made, perm, half):
    dof, source = given
    for k, block in enumerate(slot_major(dof()[...])):
        perm[rows_of(k), :] = block
        half[rows_of(k), :] = mm(block, source()[...]).astype(BF16)
    for k in range(4):
        made[0].ref[rows_of(k), :] = mm(half[rows_of(k), :], perm[...], NT).astype(BF16)
        made[0].send_rows(CAP)


def plane_rows(given, made):
    x = lax.rem(lax.axis_index("dev"), N_X)
    for i, block in enumerate(given):
        at = lax.rem(x + (N_X - i), N_X) * 32
        made[0][pl.ds(pl.multiple_of(at, 32), 32), :] = block[...]


def block_product(matrix, wide):
    both = mm(matrix[...], wide[...])
    both = both[:, :NRHS] + both[:, NRHS:]
    return [both[rows_of(k), :] for k in range(4)]


def split_into(wide, k, v):
    for i, part in enumerate(pieces(v, 2)):
        wide[rows_of(k), i * NRHS : (i + 1) * NRHS] = part


def project(rows, k, v):
    four = mm(rows[:, rows_of(k)], jnp.concatenate(pieces(v, 2), axis=1))
    return four[:128, :NRHS] + four[:128, NRHS:] + four[128:, :NRHS]


def solved_pieces(solved):
    high, low = pieces(solved[...], 2)
    return jnp.concatenate([high, high, low], axis=1)


def lane_slot(j):
    return lax.div(iota((8, 128), 1), NCL) == j


def place_basis(hs, gs, placed):
    s = lax.axis_index("sub")
    x = lax.rem(lax.axis_index("dev"), N_X)
    odd = lax.rem(s, 2)
    own = odd * 4 + x
    across, over, edge = (
        (1 - odd) * 4 + x,
        (1 - odd) * 4 + lax.rem(x + 1, 4),
        (1 - odd) * 4 + lax.rem(x + 2, 4),
    )
    places = (
        jnp.where(odd == 1, across, over),
        jnp.where(odd == 1, over, across),
        jnp.where(x > 0, odd * 4 + x - 1, edge),
        jnp.where(x < N_X - 1, odd * 4 + x + 1, edge),
    )
    placed[...] = jnp.zeros_like(placed)
    for k in range(4):
        for at, source in ((own, hs[k]), (places[k], gs[k])):
            at = pl.ds(pl.multiple_of(at * NCL, NCL), NCL)
            placed[at, rows_of(k)] = source[CAP : CAP + NCL, :]
    return s, x, own


def fill_rows(rows, placed):
    for i, part in enumerate(pieces(placed[...], 2)):
        rows[i * 128 : (i + 1) * 128, :] = part


def lane_sum(v):
    return mm(jnp.ones((8, 128), F32), v, NT, precision=EXACT)[0:1]


def rows_out(out, rows):
    full = 8 - sum(row.shape[0] for row in rows)
    out.ref[...] = jnp.concatenate(list(rows) + [jnp.zeros((full, NRHS), F32)], axis=0)


def begin(given, made, rows):
    hs, gs = given[0:4], given[4:8]
    send, sent, r_out, placed = made
    s, x, own = place_basis(hs, gs, placed.ref)
    placed.send()
    for k in range(4):
        r_out.ref[rows_of(k), :] = hs[k][0:CAP, :] + gs[k][0:CAP, :]
        r_out.send_rows(CAP)
    fill_rows(rows, placed.ref)
    total = jnp.zeros((128, NRHS), F32)
    for k in range(4):
        total = total + project(rows, k, hs[k][0:CAP, :])
    flipped = jnp.transpose(total)
    sent.ref[...] = flipped
    sent.send()
    zero = jnp.zeros((8, 128), F32)
    line = iota((8, 128), 0)
    mine = jnp.where(lane_slot(own), hs[0][CAP + NCL :, 0:128], zero)
    before = jnp.where(lane_slot(s) & (x == 0), gs[2][CAP + NCL :, 0:128], zero)
    after = jnp.where(lane_slot(s) & (x == N_X - 1), gs[3][CAP + NCL :, 0:128], zero)
    extra = jnp.where(line == 0, mine, jnp.where(line == 1, before, jnp.where(line == 2, after, zero)))
    for m in range(PEERS):
        send[m * 16 : m * 16 + 8, :] = flipped[m * 8 : m * 8 + 8, :]
        send[m * 16 + 8 : m * 16 + 16, :] = extra


def begin_local(given, made, wide):
    weights, r, inverse = given
    energy, *es = made
    weights = weights()
    for k in range(4):
        split_into(wide, k, weights[k : k + 1, :] * r()[rows_of(k), :])
    total = jnp.zeros((1, NRHS), F32)
    for k, (e, value) in enumerate(zip(es, block_product(inverse(), wide))):
        value = weights[k : k + 1, :] * value
        e.ref[...] = value
        e.send()
        total = total + jnp.sum(value * r()[rows_of(k), :], axis=0, keepdims=True)
    rows_out(energy, [total])


def three_wide(out, v):
    high, low = pieces(v, 2)
    out[:, 0:128] = high
    out[:, 128:256] = low
    out[:, 256:384] = high


def basis_tables(given, made):
    placed, schur = given
    rows, columns, images, coarse = made
    fill_rows(rows.ref, placed())
    rows.send()
    three_wide(columns.ref, jnp.transpose(placed()[...]))
    columns.send()
    both = mm(schur()[...], columns.ref[:, 0:256])
    three_wide(images.ref, both[:, :128] + both[:, 128:])
    images.send()
    four = mm(rows.ref[...], images.ref[:, 0:256])
    coarse.ref[...] = four[:128, :128] + four[:128, 128:] + four[128:, :128]


def layout(m):
    s, x = divmod(m, N_X)
    odd = s % 2
    keep = [odd * 4 + x, (1 - odd) * 4 + x]
    keep += [odd * 4 + v for v in (x - 1, x + 1) if 0 <= v < N_X]
    moves = []
    other = s + 1 if odd else s - 1
    if 0 <= other < N_SUB:
        moves.append(((1 - odd) * 4 + (x + 1) % 4, other // 2, (1 - odd) * 4 + x))
    if x in (0, N_X - 1):
        moves.append(((1 - odd) * 4 + (x + 2) % 4, 4 if x == 0 else 5, s))
    return s // 2, keep, moves


def lanes_in(slots):
    at = lax.div(iota((8, 128), 1), NCL)
    hit = at == slots[0]
    for j in slots[1:]:
        hit = hit | (at == j)
    return hit


def roll_slots(v, shift):
    shift = (shift * NCL) % 128
    return pltpu.roll(v, shift, 1) if shift else v


def spread(tiles):
    groups = [jnp.zeros((8, 128), F32) for _ in range(6)]
    for m in range(PEERS):
        base, keep, moves = layout(m)
        tile = tiles(m)
        groups[base] = groups[base] + jnp.where(lanes_in(keep), tile, 0.0)
        for here, group, there in moves:
            part = roll_slots(jnp.where(lanes_in([here]), tile, 0.0), there - here)
            groups[group] = groups[group] + part
    return jnp.concatenate(groups, axis=1)


def fold(groups, pick, out):
    three = mm(jnp.concatenate(pieces(groups, 3), axis=0), pick, NT)
    result = three[0:8] + three[8:16] + three[16:24]
    for z in range(N_Z):
        out[z * 8 : z * 8 + 8, :] = result


def gather_first(given, made):
    received = given[0]
    out, pick_out = made
    groups = spread(lambda m: received[m * 16 : m * 16 + 8, :])
    ids = [jnp.zeros((8, 128), F32) for _ in range(6)]
    for m in range(PEERS):
        extra = received[m * 16 + 8 : m * 16 + 16, :]
        base = m // 8
        ids[base] = ids[base] + extra
        ids[4] = ids[4] + extra
        ids[5] = ids[5] + extra
    index = jnp.concatenate(
        [ids[0][0:1], ids[1][0:1], ids[2][0:1], ids[3][0:1], ids[4][1:2], ids[5][2:3]], axis=1
    ).astype(jnp.int32)
    pick = jnp.where(iota((NC, 768), 0) == index, 1.0, 0.0).astype(BF16)
    pick_out[...] = pick
    fold(groups, pick, out)


def gather_again(given, made):
    received, pick = given
    groups = spread(lambda m: received[m * 8 : m * 8 + 8, :])
    fold(groups, pick[...], made[0])


def coarse_solve(given, made):
    received, plane = given
    out = made[0]
    rhs = received[0:8, :]
    for z in range(1, N_Z):
        rhs = rhs + received[z * 8 : z * 8 + 8, :]
    solved = mm(rhs, plane[...], NT, precision=EXACT)
    for z in range(N_Z):
        out[z * 8 : z * 8 + 8, :] = solved


def give_back(given, made):
    received, pick = given
    out = made[0]
    solved = jnp.concatenate([received[z * 8 : z * 8 + 8, :] for z in range(N_Z)], axis=1)
    three = mm(jnp.concatenate(pieces(solved, 3), axis=0), pick[...])
    every = three[0:8] + three[8:16] + three[16:24]
    groups = [every[:, g * 128 : (g + 1) * 128] for g in range(6)]
    for m in range(PEERS):
        base, keep, moves = layout(m)
        tile = jnp.where(lanes_in(keep), groups[base], 0.0)
        for here, group, there in moves:
            tile = jnp.where(lanes_in([here]), roll_slots(groups[group], here - there), tile)
        out[m * 8 : m * 8 + 8, :] = tile


def middle(schur, rows, halves, local_out, image, send_local, wide):
    for k in range(4):
        local = halves[k]()[...] + halves[k + 4]()[...]
        local_out.ref[rows_of(k), :] = local
        local_out.send_rows(CAP)
        split_into(wide, k, local)
    total = jnp.zeros((128, NRHS), F32)
    energy = jnp.zeros((1, NRHS), F32)
    for k, value in enumerate(block_product(schur(), wide)):
        image.ref[rows_of(k), :] = value
        image.send_rows(CAP)
        energy = energy + jnp.sum(value * local_out.ref[rows_of(k), :], axis=0, keepdims=True)
        total = total + project(rows(), k, value)
    send_local.ref[0:NRHS, :] = jnp.transpose(total)
    return energy


def first_middle(given, made, wide):
    schur, rows, *halves = given
    local_out, image, send_local, energy = made
    rows_out(energy, [middle(schur, rows, halves, local_out, image, send_local, wide)])


def energies(solved, sent, send_local, coarse):
    cross = 2.0 * send_local + mm(solved, coarse, NT, precision=EXACT)
    return lane_sum(solved * sent), lane_sum(solved * cross)


def first_send(given, made):
    solved, send_local, coarse = given
    product = mm(solved[...], coarse[...], NT, precision=EXACT)
    made[0][...] = send_local[...] + product


def add_coarse(given, made):
    solved, images, image = given
    kept, *outs = made
    kept.ref[...] = solved[...]
    kept.send()
    back = solved_pieces(solved)
    for k, out in enumerate(outs):
        rows = rows_of(k)
        out.ref[...] = image()[rows, :] + mm(images()[rows, :], back, NT)
        out.send()


def first_direction(given, made):
    add_coarse(given, made)


def second_direction(given, made):
    add_coarse(given, made)


def first_energies(given, made):
    energy, other, solved, sent, send_local, coarse = given
    norm, curvature = energies(solved()[...], sent()[...], send_local()[...], coarse()[...])
    rows_out(made[0], [energy()[0:1, :] + norm, other()[0:1, :] + curvature])


def second_local(given, made, wide):
    weights, *halves = given[:9]
    inverse, dots = given[9:]
    t_out, dots_out, *es = made
    weights = weights()
    for k in range(4):
        t = halves[k]()[...] + halves[k + 4]()[...]
        t_out.ref[rows_of(k), :] = t
        t_out.send_rows(CAP)
        split_into(wide, k, weights[k : k + 1, :] * t)
    total = jnp.zeros((1, NRHS), F32)
    for k, (e, value) in enumerate(zip(es, block_product(inverse(), wide))):
        value = weights[k : k + 1, :] * value
        e.ref[...] = value
        e.send()
        total = total + jnp.sum(value * t_out.ref[rows_of(k), :], axis=0, keepdims=True)
    rows_out(dots_out, [dots()[0:2, :], total])


def second_middle(given, made, wide):
    schur, rows, dots, *halves = given
    local_out, image, packed = made
    energy = middle(schur, rows, halves, local_out, image, packed, wide)
    tail = jnp.concatenate([dots()[0:3, :], energy, jnp.zeros((4, NRHS), F32)], axis=0)
    packed.ref[NRHS : NRHS + 8, :] = tail[:, 0:128]
    packed.ref[NRHS + 8 : NRHS + 16, :] = tail[:, 128:]


def dots_send(given, made):
    solved, sent, packed, coarse = given
    first, second = energies(solved[...], sent[...], packed[0:NRHS, :], coarse[...])
    dots = jnp.concatenate([packed[NRHS : NRHS + 8, :], packed[NRHS + 8 :, :]], axis=1)
    values = (dots[0:1, :], dots[1:2, :], dots[2:3, :] + first, dots[3:4, :] + second)
    tile = jnp.concatenate([v[:, :128] for v in values] + [v[:, 128:] for v in values], axis=0)
    for m in range(PEERS):
        made[0][m * 8 : m * 8 + 8, :] = tile


def add_plane(given, made):
    received, out = given[0], made[0]
    total = received[0:8, :]
    for m in range(1, PEERS):
        total = total + received[m * 8 : m * 8 + 8, :]
    for z in range(N_Z):
        out[z * 8 : z * 8 + 8, :] = total


def vectors(given, made):
    columns, solved, local, solved_too, local_too = given
    for out, back, v in ((made[0], solved, local), (made[1], solved_too, local_too)):
        back = solved_pieces(back())
        for k in range(4):
            rows = rows_of(k)
            out.ref[rows, :] = v()[rows, :] + mm(columns()[rows, :], back, NT)
            out.send_rows(CAP)


def finish(given, made, perm_t, wide):
    received, dof, p, v, r, t, *halves = given
    for k, block in enumerate(unknown_major(dof[...])):
        perm_t[:, rows_of(k)] = block
    total = received[0:8, :]
    for z in range(1, N_Z):
        total = total + received[z * 8 : z * 8 + 8, :]
    norm, curvature, g, h = (
        jnp.concatenate([total[i : i + 1], total[i + 4 : i + 5]], axis=1) for i in range(4)
    )
    step = norm / curvature
    scaled = step * g
    grown = scaled / curvature
    next_norm = (grown - 1.0) * norm
    next_curvature = step * (step * h) - grown * scaled
    next_step = next_norm / next_curvature
    both = step + next_step * grown
    cross = next_step * step
    for k in range(4):
        rows = rows_of(k)
        split_into(wide.at[:, 0 : 2 * NRHS], k, both * p[rows, :] - cross * v[rows, :])
    for k in range(4):
        rows = rows_of(k)
        w = halves[k][...] + halves[k + 4][...]
        value = r[rows, :] - both * t[rows, :] + cross * w
        split_into(wide.at[:, 2 * NRHS : 4 * NRHS], k, value)
    for j, out in enumerate(made):
        two = mm(perm_t[...], wide[:, 2 * j * NRHS : 2 * (j + 1) * NRHS])
        out[...] = two[:, :NRHS] + two[:, NRHS:]


PLANES = [[s * N_DEV + z * N_X + x for s in range(N_SUB) for x in range(N_X)] for z in range(N_Z)]
LINES = [[z * N_X + x for z in range(N_Z)] for x in range(N_X)]


def over_plane(v):
    return lax.all_to_all(v, ("sub", "dev"), 0, 0, tiled=True, axis_index_groups=PLANES)


def over_line(v):
    return lax.all_to_all(v, "dev", 0, 0, tiled=True, axis_index_groups=LINES)


def ring(v, axis, count, shift):
    return lax.ppermute(v, axis, [(i, (i + shift) % count) for i in range(count)])


def halo(blocks):
    return [
        ring(blocks[1], "sub", N_SUB, 1),
        ring(blocks[0], "sub", N_SUB, -1),
        ring(blocks[3], "dev", N_DEV, 1),
        ring(blocks[2], "dev", N_DEV, -1),
    ]


def together(first, *others):
    return lax.optimization_barrier((first, *others))


def small(body, outs, ins, smem=(), flops=LONG):
    return run(
        body,
        outs,
        ins,
        smem=smem,
        near=[i for i in range(len(ins)) if i not in smem],
        near_outs=range(len(outs)),
        limit=12,
        flops=flops,
    )


def shards(
    load, schur, local_inverse, coarse_basis, coarse_inverse, dof_lists, coarse_map, stiffness
):
    dof = dof_lists[0]
    block = shape(CAP, NRHS)
    vector = shape(NI, NRHS)
    square = shape(NI, NI, dtype=BF16)
    lanes = shape(NRHS, 128)
    table = shape(NI, 384, dtype=BF16)
    wide = pltpu.VMEM((NI, 2 * NRHS), BF16)
    half = pltpu.VMEM((NI, NI), BF16)
    big = 2 * NI * NI * NRHS

    *hs, weights = run(
        prepare,
        [shape(HROWS, NRHS)] * 4 + [shape(8, NRHS)],
        [dof, coarse_basis, load, coarse_map, stiffness.reshape(1, -1)],
        near_outs=range(4),
        scratch=[pltpu.VMEM((NI, 2 * NRHS + 128), BF16)],
        flops=3 * big,
    )
    gs = halo(hs)
    (schur_s,) = run(
        order, [square], [dof, schur], scratch=[half, half], limit=59, flops=8 * big
    )
    coarse_inverse, schur_s = together(coarse_inverse, schur_s)
    planes = [
        lax.ppermute(
            coarse_inverse,
            "dev",
            [(z * N_X + x, z * N_X + (x + i) % N_X) for z in range(N_Z) for x in range(N_X)],
        )
        for i in range(1, N_X)
    ]
    schur_s, *gs = together(schur_s, *gs)
    send, sent, r, placed = run(
        begin,
        [shape(PEERS * 16, 128), lanes, vector, shape(128, NI)],
        [*hs, *gs],
        near=range(8),
        near_outs=(0,),
        limit=60.2,
        scratch=[pltpu.VMEM((256, NI), BF16)],
        flops=big // 2,
    )
    (inverse_s,) = run(order, [square], [dof, local_inverse], scratch=[half, half], flops=8 * big)
    (plane,) = small(plane_rows, [shape(128, NC)], [coarse_inverse, *planes], flops=0)
    received, inverse_s, plane = together(over_plane(send), inverse_s, plane)
    line, pick = small(gather_first, [shape(N_Z * 8, NC), shape(NC, 768, dtype=BF16)], [received])

    def coarse_middle(received):
        (part,) = small(coarse_solve, [shape(N_Z * 8, 128)], [received, plane])
        return part

    def coarse_end(part):
        (back,) = small(give_back, [shape(PEERS * 8, 128)], [part, pick])
        return back

    energy, *es = run(
        begin_local,
        [shape(8, NRHS)] + [block] * 4,
        [weights, r, inverse_s],
        scratch=[wide],
        flops=2 * big,
    )
    es_halo = halo(es)
    received, energy = together(over_line(line), energy)
    part = coarse_middle(received)
    placed, *es_halo = together(placed, *es_halo)
    rows, columns, images, coarse = run(
        basis_tables,
        [shape(256, NI, dtype=BF16), table, table, shape(128, 128)],
        [placed, schur_s],
        flops=big,
    )
    received, rows, columns, images, coarse = together(
        over_line(part), rows, columns, images, coarse
    )
    back = coarse_end(received)
    local, image, send_local, other = run(
        first_middle,
        [vector, vector, lanes, shape(8, NRHS)],
        [schur_s, rows, *es, *es_halo],
        scratch=[wide],
        flops=2 * big,
    )
    solved = over_plane(back)
    (sending,) = small(first_send, [lanes], [solved, send_local, coarse])
    solved, send = together(solved, sending)
    kept, *qs = run(
        first_direction,
        [lanes] + [block] * 4,
        [solved, images, image],
        near=(0,),
        flops=big,
    )
    qs_halo = halo(qs)
    received, *qs = together(over_plane(send), *qs)
    (line,) = small(gather_again, [shape(N_Z * 8, NC)], [received, pick])
    (dots,) = run(
        first_energies, [shape(8, NRHS)], [energy, other, kept, sent, send_local, coarse]
    )
    received, dots = together(over_line(line), dots)
    part = coarse_middle(received)
    _, inverse_s = together(part, inverse_s)
    t, dots, *es = run(
        second_local,
        [vector, shape(8, NRHS)] + [block] * 4,
        [weights, *qs, *qs_halo, inverse_s, dots],
        scratch=[wide],
        flops=2 * big,
    )
    es_halo = halo(es)
    received, dots = together(over_line(part), dots)
    back = coarse_end(received)
    local_too, image, packed = run(
        second_middle,
        [vector, vector, shape(NRHS + 16, 128)],
        [schur_s, rows, dots, *es, *es_halo],
        scratch=[wide],
        flops=2 * big,
    )
    solved = over_plane(back)
    (send,) = small(dots_send, [lanes], [solved, sending, packed, coarse])
    solved, send = together(solved, send)
    kept_too, *us = run(
        second_direction,
        [lanes] + [block] * 4,
        [solved, images, image],
        near=(0,),
        flops=big,
    )
    us_halo = halo(us)
    received, *us = together(over_plane(send), *us)
    (line,) = small(add_plane, [shape(N_Z * 8, 128)], [received])
    line, local_too = together(line, local_too)
    p, v = run(
        vectors,
        [vector, vector],
        [columns, kept, local, kept_too, local_too],
        flops=big // 2,
    )
    received, p, v = together(over_line(line), p, v)
    return tuple(
        run(
            finish,
            [vector, vector],
            [received, dof, p, v, r, t, *us, *us_halo],
            near=range(14),
            near_outs=(0, 1),
            limit=30,
            scratch=[half, pltpu.VMEM((NI, 4 * NRHS), BF16)],
            flops=4 * big,
        )
    )


def solution(mesh):
    placed = (
        P(("sub", "dev"), None),
        P(("sub", "dev"), None),
        P(("sub", "dev"), None),
        P(("sub", "dev"), None),
        P("dev", None),
        P(("sub", "dev"), None, None),
        P(("sub", "dev"), None),
        P(),
    )
    return jax.shard_map(
        shards,
        mesh=mesh,
        in_specs=placed,
        out_specs=(P(("sub", "dev"), None), P(("sub", "dev"), None)),
        check_vma=False,
    )
```

```python
import jax
import jax.numpy as jnp
import numpy as np
from jax import lax
from jax.experimental import pallas as pl
from jax.experimental.pallas import tpu as pltpu
from jax.sharding import PartitionSpec as P

F32, BF16 = jnp.float32, jnp.bfloat16
EXACT = lax.Precision.HIGHEST
NI, NRHS, NCL, CAP, NC = 1024, 256, 16, 256, 1024
N_SUB, N_DEV, N_X, N_Z = 8, 32, 4, 8
PEERS = N_SUB * N_X
MIB = 1 << 20
LONG = 20 << 30
NN = (((1,), (0,)), ((), ()))
NT = (((1,), (1,)), ((), ()))


def mm(a, b, dims=NN, precision=None):
    return lax.dot_general(a, b, dims, precision=precision, preferred_element_type=F32)


def pieces(v, count):
    out = []
    for i in range(count):
        part = v.astype(BF16)
        out.append(part)
        if i + 1 < count:
            v = v - part.astype(F32)
    return out


def shape(*dims, dtype=F32):
    return jax.ShapeDtypeStruct(dims, dtype)


CHUNK = 256 << 10


def start_copies(source, target, arrived, rows, itemsize):
    size = int(np.prod(target.shape[1:])) * itemsize
    step = max(16, CHUNK // size // 16 * 16)
    for first in range(0, rows, step):
        at = pl.ds(first, min(step, rows - first))
        pltpu.make_async_copy(source.at[at], target.at[at], arrived).start()


class Operand:
    def __init__(self, source, target, arrived):
        self.target, self.waited = target, False
        self.copy = pltpu.make_async_copy(source, target, arrived)
        start_copies(source, target, arrived, target.shape[0], target.dtype.itemsize)

    def __call__(self):
        if not self.waited:
            self.copy.wait()
            self.waited = True
        return self.target


class Result:
    def __init__(self, source, target, arrived):
        self.ref, self.target, self.arrived, self.sent = source, target, arrived, 0
        self.copy = pltpu.make_async_copy(source, target, arrived)

    def send(self):
        if not self.sent:
            self.sent = self.ref.shape[0]
            start_copies(self.ref, self.target, self.arrived, self.sent, self.ref.dtype.itemsize)

    def send_rows(self, count):
        at = pl.ds(self.sent, count)
        pltpu.make_async_copy(self.ref.at[at], self.target.at[at], self.arrived).start()
        self.sent += count


def run(body, outs, ins, smem=(), near=(), near_outs=(), part=None, scratch=(), limit=61, flops=0):
    part = part or {}
    places = {i: pltpu.SMEM for i in smem} | {i: pltpu.VMEM for i in near}
    far = [i for i in range(len(ins)) if i not in places]
    far_outs = [i for i in range(len(outs)) if i not in near_outs]
    rows = {i: part.get(i, (0, ins[i].shape[0])) for i in far}
    buffers = [pltpu.VMEM((rows[i][1],) + ins[i].shape[1:], ins[i].dtype) for i in far]
    buffers += [pltpu.VMEM(outs[i].shape, outs[i].dtype) for i in far_outs]
    count = len(buffers)
    size = sum(int(np.prod(a.shape)) * a.dtype.itemsize for a in list(ins) + list(outs))

    def kernel(*refs):
        given, refs = list(refs[: len(ins)]), refs[len(ins) :]
        made, refs = list(refs[: len(outs)]), refs[len(outs) :]
        held, arrived, rest = refs[:count], refs[count], refs[count + 1 :]
        for n, i in enumerate(far):
            begin, length = rows[i]
            source = given[i] if length == ins[i].shape[0] else given[i].at[pl.ds(begin, length)]
            given[i] = Operand(source, held[n], arrived.at[n])
        for n, i in enumerate(far_outs, len(far)):
            made[i] = Result(held[n], made[i], arrived.at[n])
        body(given, made, *rest)
        for i in far_outs:
            made[i].send()
        for i in far:
            given[i]()
        for i in far_outs:
            made[i].copy.wait()

    return pl.pallas_call(
        kernel,
        out_shape=list(outs),
        in_specs=[pl.BlockSpec(memory_space=places.get(i, pl.ANY)) for i in range(len(ins))],
        out_specs=[
            pl.BlockSpec(memory_space=pltpu.VMEM if i in near_outs else pl.ANY)
            for i in range(len(outs))
        ],
        scratch_shapes=buffers + [pltpu.SemaphoreType.DMA((max(count, 1),))] + list(scratch),
        compiler_params=pltpu.CompilerParams(vmem_limit_bytes=int(limit * MIB)),
        cost_estimate=pl.CostEstimate(flops=flops, bytes_accessed=size, transcendentals=0),
        name=body.__name__,
    )(*ins)


def slot_weights(stiffness):
    p = lax.axis_index("sub") * N_DEV + lax.axis_index("dev")
    lanes = iota((1, NRHS), 1)

    def value(q):
        q = jnp.clip(q, 0, N_SUB * N_DEV - 1)
        one = jnp.sum(jnp.where(lanes == q, stiffness, 0.0), axis=1, keepdims=True)
        return jnp.broadcast_to(one, (1, NRHS))

    own = value(p)
    return [own / (own + value(p + shift)) for shift in (-N_DEV, N_DEV, -1, 1)]


def iota(dims, axis):
    return lax.broadcasted_iota(jnp.int32, dims, axis)


def slot_major(dof):
    wide = jnp.concatenate([dof.astype(F32), jnp.zeros((4, CAP), F32)], axis=0)
    columns = jnp.transpose(wide)
    lanes = iota((CAP, NI), 1).astype(F32)
    return (jnp.where(columns[:, k : k + 1] == lanes, 1.0, 0.0).astype(BF16) for k in range(4))


def unknown_major(dof):
    rows = iota((NI, CAP), 0)
    return [jnp.where(rows == dof[k : k + 1, :], 1.0, 0.0).astype(BF16) for k in range(4)]


def rows_of(k):
    return slice(k * CAP, (k + 1) * CAP)


HROWS = CAP + NCL + 8


def prepare(given, made, wide):
    dof, basis, load, names, stiffness = given
    *hs, weights_out = made
    blocks = slot_major(dof()[...])
    turned = jnp.transpose(jnp.concatenate([basis()[...], jnp.zeros((48, NI), F32)], axis=0))
    high, low = pieces(turned, 2)
    wide[:, 2 * NRHS : 2 * NRHS + 64] = high
    wide[:, 2 * NRHS + 64 :] = low
    for i, part in enumerate(pieces(load()[...], 2)):
        wide[:, i * NRHS : (i + 1) * NRHS] = part
    tiled = jnp.where(
        lax.rem(iota((NCL, NRHS), 1), NCL) == iota((NCL, NRHS), 0), 1.0, 0.0
    ).astype(BF16)
    ids = pieces(jnp.broadcast_to(names()[...].astype(F32), (8, NCL)), 2)
    ids = mm(ids[0], tiled) + mm(ids[1], tiled)
    weights = slot_weights(stiffness()[...])
    weights_out.ref[...] = jnp.concatenate(weights + [jnp.zeros((4, NRHS), F32)], axis=0)
    weights_out.send()
    for k, h in enumerate(hs):
        both = mm(next(blocks), wide[...])
        h[0:CAP, :] = both[:, :NRHS] + both[:, NRHS : 2 * NRHS]
        own = jnp.transpose(both[:, 2 * NRHS :])
        h[CAP : CAP + NCL, :] = weights[k] * (own[0:NCL] + own[64 : 64 + NCL])
        h[CAP + NCL :, :] = ids


def order(given, made, perm, half):
    dof, source = given
    for k, block in enumerate(slot_major(dof()[...])):
        perm[rows_of(k), :] = block
        half[rows_of(k), :] = mm(block, source()[...]).astype(BF16)
    for k in range(4):
        made[0].ref[rows_of(k), :] = mm(half[rows_of(k), :], perm[...], NT).astype(BF16)
        made[0].send_rows(CAP)


def plane_rows(given, made):
    x = lax.rem(lax.axis_index("dev"), N_X)
    for i, block in enumerate(given):
        at = lax.rem(x + (N_X - i), N_X) * 32
        made[0][pl.ds(pl.multiple_of(at, 32), 32), :] = block[...]


def block_product(matrix, wide):
    both = mm(matrix[...], wide[...])
    both = both[:, :NRHS] + both[:, NRHS:]
    return [both[rows_of(k), :] for k in range(4)]


def split_into(wide, k, v):
    for i, part in enumerate(pieces(v, 2)):
        wide[rows_of(k), i * NRHS : (i + 1) * NRHS] = part


def project(rows, k, v):
    four = mm(rows[:, rows_of(k)], jnp.concatenate(pieces(v, 2), axis=1))
    return four[:128, :NRHS] + four[:128, NRHS:] + four[128:, :NRHS]


def solved_pieces(solved):
    high, low = pieces(solved[...], 2)
    return jnp.concatenate([high, high, low], axis=1)


def lane_slot(j):
    return lax.div(iota((8, 128), 1), NCL) == j


def place_basis(hs, gs, placed):
    s = lax.axis_index("sub")
    x = lax.rem(lax.axis_index("dev"), N_X)
    odd = lax.rem(s, 2)
    own = odd * 4 + x
    across, over, edge = (
        (1 - odd) * 4 + x,
        (1 - odd) * 4 + lax.rem(x + 1, 4),
        (1 - odd) * 4 + lax.rem(x + 2, 4),
    )
    places = (
        jnp.where(odd == 1, across, over),
        jnp.where(odd == 1, over, across),
        jnp.where(x > 0, odd * 4 + x - 1, edge),
        jnp.where(x < N_X - 1, odd * 4 + x + 1, edge),
    )
    placed[...] = jnp.zeros_like(placed)
    for k in range(4):
        for at, source in ((own, hs[k]), (places[k], gs[k])):
            at = pl.ds(pl.multiple_of(at * NCL, NCL), NCL)
            placed[at, rows_of(k)] = source[CAP : CAP + NCL, :]
    return s, x, own


def fill_rows(rows, placed):
    for i, part in enumerate(pieces(placed[...], 2)):
        rows[i * 128 : (i + 1) * 128, :] = part


def lane_sum(v):
    return mm(jnp.ones((8, 128), F32), v, NT, precision=EXACT)[0:1]


def rows_out(out, rows):
    full = 8 - sum(row.shape[0] for row in rows)
    out.ref[...] = jnp.concatenate(list(rows) + [jnp.zeros((full, NRHS), F32)], axis=0)


def begin(given, made, rows):
    hs, gs = given[0:4], given[4:8]
    send, sent, r_out, placed = made
    s, x, own = place_basis(hs, gs, placed.ref)
    placed.send()
    for k in range(4):
        r_out.ref[rows_of(k), :] = hs[k][0:CAP, :] + gs[k][0:CAP, :]
        r_out.send_rows(CAP)
    fill_rows(rows, placed.ref)
    total = jnp.zeros((128, NRHS), F32)
    for k in range(4):
        total = total + project(rows, k, hs[k][0:CAP, :])
    flipped = jnp.transpose(total)
    sent.ref[...] = flipped
    sent.send()
    zero = jnp.zeros((8, 128), F32)
    line = iota((8, 128), 0)
    mine = jnp.where(lane_slot(own), hs[0][CAP + NCL :, 0:128], zero)
    before = jnp.where(lane_slot(s) & (x == 0), gs[2][CAP + NCL :, 0:128], zero)
    after = jnp.where(lane_slot(s) & (x == N_X - 1), gs[3][CAP + NCL :, 0:128], zero)
    extra = jnp.where(line == 0, mine, jnp.where(line == 1, before, jnp.where(line == 2, after, zero)))
    for m in range(PEERS):
        send[m * 16 : m * 16 + 8, :] = flipped[m * 8 : m * 8 + 8, :]
        send[m * 16 + 8 : m * 16 + 16, :] = extra


def begin_local(given, made, wide):
    weights, r, inverse = given
    energy, *es = made
    weights = weights()
    for k in range(4):
        split_into(wide, k, weights[k : k + 1, :] * r()[rows_of(k), :])
    total = jnp.zeros((1, NRHS), F32)
    for k, (e, value) in enumerate(zip(es, block_product(inverse(), wide))):
        value = weights[k : k + 1, :] * value
        e.ref[...] = value
        e.send()
        total = total + jnp.sum(value * r()[rows_of(k), :], axis=0, keepdims=True)
    rows_out(energy, [total])


def three_wide(out, v):
    high, low = pieces(v, 2)
    out[:, 0:128] = high
    out[:, 128:256] = low
    out[:, 256:384] = high


def basis_tables(given, made):
    placed, schur = given
    rows, columns, images, coarse = made
    fill_rows(rows.ref, placed())
    rows.send()
    three_wide(columns.ref, jnp.transpose(placed()[...]))
    columns.send()
    both = mm(schur()[...], columns.ref[:, 0:256])
    three_wide(images.ref, both[:, :128] + both[:, 128:])
    images.send()
    four = mm(rows.ref[...], images.ref[:, 0:256])
    coarse.ref[...] = four[:128, :128] + four[:128, 128:] + four[128:, :128]


def layout(m):
    s, x = divmod(m, N_X)
    odd = s % 2
    keep = [odd * 4 + x, (1 - odd) * 4 + x]
    keep += [odd * 4 + v for v in (x - 1, x + 1) if 0 <= v < N_X]
    moves = []
    other = s + 1 if odd else s - 1
    if 0 <= other < N_SUB:
        moves.append(((1 - odd) * 4 + (x + 1) % 4, other // 2, (1 - odd) * 4 + x))
    if x in (0, N_X - 1):
        moves.append(((1 - odd) * 4 + (x + 2) % 4, 4 if x == 0 else 5, s))
    return s // 2, keep, moves


def lanes_in(slots):
    at = lax.div(iota((8, 128), 1), NCL)
    hit = at == slots[0]
    for j in slots[1:]:
        hit = hit | (at == j)
    return hit


def roll_slots(v, shift):
    shift = (shift * NCL) % 128
    return pltpu.roll(v, shift, 1) if shift else v


def spread(tiles):
    groups = [jnp.zeros((8, 128), F32) for _ in range(6)]
    for m in range(PEERS):
        base, keep, moves = layout(m)
        tile = tiles(m)
        groups[base] = groups[base] + jnp.where(lanes_in(keep), tile, 0.0)
        for here, group, there in moves:
            part = roll_slots(jnp.where(lanes_in([here]), tile, 0.0), there - here)
            groups[group] = groups[group] + part
    return jnp.concatenate(groups, axis=1)


def fold(groups, pick, out):
    three = mm(jnp.concatenate(pieces(groups, 3), axis=0), pick, NT)
    result = three[0:8] + three[8:16] + three[16:24]
    for z in range(N_Z):
        out[z * 8 : z * 8 + 8, :] = result


def gather_first(given, made):
    received = given[0]
    out, pick_out = made
    groups = spread(lambda m: received[m * 16 : m * 16 + 8, :])
    ids = [jnp.zeros((8, 128), F32) for _ in range(6)]
    for m in range(PEERS):
        extra = received[m * 16 + 8 : m * 16 + 16, :]
        base = m // 8
        ids[base] = ids[base] + extra
        ids[4] = ids[4] + extra
        ids[5] = ids[5] + extra
    index = jnp.concatenate(
        [ids[0][0:1], ids[1][0:1], ids[2][0:1], ids[3][0:1], ids[4][1:2], ids[5][2:3]], axis=1
    ).astype(jnp.int32)
    pick = jnp.where(iota((NC, 768), 0) == index, 1.0, 0.0).astype(BF16)
    pick_out[...] = pick
    fold(groups, pick, out)


def gather_again(given, made):
    received, pick = given
    groups = spread(lambda m: received[m * 8 : m * 8 + 8, :])
    fold(groups, pick[...], made[0])


def coarse_solve(given, made):
    received, plane = given
    out = made[0]
    rhs = received[0:8, :]
    for z in range(1, N_Z):
        rhs = rhs + received[z * 8 : z * 8 + 8, :]
    solved = mm(rhs, plane[...], NT, precision=EXACT)
    for z in range(N_Z):
        out[z * 8 : z * 8 + 8, :] = solved


def give_back(given, made):
    received, pick = given
    out = made[0]
    solved = jnp.concatenate([received[z * 8 : z * 8 + 8, :] for z in range(N_Z)], axis=1)
    three = mm(jnp.concatenate(pieces(solved, 3), axis=0), pick[...])
    every = three[0:8] + three[8:16] + three[16:24]
    groups = [every[:, g * 128 : (g + 1) * 128] for g in range(6)]
    for m in range(PEERS):
        base, keep, moves = layout(m)
        tile = jnp.where(lanes_in(keep), groups[base], 0.0)
        for here, group, there in moves:
            tile = jnp.where(lanes_in([here]), roll_slots(groups[group], here - there), tile)
        out[m * 8 : m * 8 + 8, :] = tile


def middle(schur, rows, halves, local_out, image, send_local, wide):
    for k in range(4):
        local = halves[k]()[...] + halves[k + 4]()[...]
        local_out.ref[rows_of(k), :] = local
        local_out.send_rows(CAP)
        split_into(wide, k, local)
    total = jnp.zeros((128, NRHS), F32)
    energy = jnp.zeros((1, NRHS), F32)
    for k, value in enumerate(block_product(schur(), wide)):
        image.ref[rows_of(k), :] = value
        image.send_rows(CAP)
        energy = energy + jnp.sum(value * local_out.ref[rows_of(k), :], axis=0, keepdims=True)
        total = total + project(rows(), k, value)
    send_local.ref[0:NRHS, :] = jnp.transpose(total)
    return energy


def first_middle(given, made, wide):
    schur, rows, *halves = given
    local_out, image, send_local, energy = made
    rows_out(energy, [middle(schur, rows, halves, local_out, image, send_local, wide)])


def energies(solved, sent, send_local, coarse):
    cross = 2.0 * send_local + mm(solved, coarse, NT, precision=EXACT)
    return lane_sum(solved * sent), lane_sum(solved * cross)


def first_send(given, made):
    solved, send_local, coarse = given
    product = mm(solved[...], coarse[...], NT, precision=EXACT)
    made[0][...] = send_local[...] + product


def held(v):
    return v() if isinstance(v, Operand) else v


def add_coarse(given, made):
    solved, images, image = given
    kept, *outs = made
    kept.ref[...] = solved[...]
    kept.send()
    back = solved_pieces(solved)
    for k, out in enumerate(outs):
        rows = rows_of(k)
        out.ref[...] = image()[rows, :] + mm(images()[rows, :], back, NT)
        out.send()


def first_direction(given, made):
    add_coarse(given, made)


def second_direction(given, made):
    add_coarse(given, made)


def first_energies(given, made):
    energy, other, solved, sent, send_local, coarse = given
    norm, curvature = energies(solved()[...], sent()[...], send_local()[...], coarse()[...])
    rows_out(made[0], [energy()[0:1, :] + norm, other()[0:1, :] + curvature])


def second_local(given, made, wide):
    weights, *halves = given[:9]
    inverse, dots = given[9:]
    t_out, dots_out, *es = made
    weights = weights()
    for k in range(4):
        t = halves[k]()[...] + halves[k + 4]()[...]
        t_out.ref[rows_of(k), :] = t
        t_out.send_rows(CAP)
        split_into(wide, k, weights[k : k + 1, :] * t)
    total = jnp.zeros((1, NRHS), F32)
    for k, (e, value) in enumerate(zip(es, block_product(inverse(), wide))):
        value = weights[k : k + 1, :] * value
        e.ref[...] = value
        e.send()
        total = total + jnp.sum(value * t_out.ref[rows_of(k), :], axis=0, keepdims=True)
    rows_out(dots_out, [dots()[0:2, :], total])


def second_middle(given, made, wide):
    schur, rows, dots, *halves = given
    local_out, image, packed = made
    energy = middle(schur, rows, halves, local_out, image, packed, wide)
    tail = jnp.concatenate([dots()[0:3, :], energy, jnp.zeros((4, NRHS), F32)], axis=0)
    packed.ref[NRHS : NRHS + 8, :] = tail[:, 0:128]
    packed.ref[NRHS + 8 : NRHS + 16, :] = tail[:, 128:]


def dots_send(given, made):
    solved, sent, packed, coarse = given
    first, second = energies(solved[...], sent[...], packed[0:NRHS, :], coarse[...])
    dots = jnp.concatenate([packed[NRHS : NRHS + 8, :], packed[NRHS + 8 :, :]], axis=1)
    values = (dots[0:1, :], dots[1:2, :], dots[2:3, :] + first, dots[3:4, :] + second)
    tile = jnp.concatenate([v[:, :128] for v in values] + [v[:, 128:] for v in values], axis=0)
    for m in range(PEERS):
        made[0][m * 8 : m * 8 + 8, :] = tile


def add_plane(given, made):
    received, out = given[0], made[0]
    total = received[0:8, :]
    for m in range(1, PEERS):
        total = total + received[m * 8 : m * 8 + 8, :]
    for z in range(N_Z):
        out[z * 8 : z * 8 + 8, :] = total


def vectors(given, made):
    columns, solved, local, solved_too, local_too = given
    for out, back, v in ((made[0], solved, local), (made[1], solved_too, local_too)):
        back = solved_pieces(back())
        for k in range(4):
            rows = rows_of(k)
            out.ref[rows, :] = v()[rows, :] + mm(columns()[rows, :], back, NT)
            out.send_rows(CAP)


def finish(given, made, perm_t, wide):
    received, dof, p, v, r, t, *halves = given
    for k, block in enumerate(unknown_major(dof()[...])):
        perm_t[:, rows_of(k)] = block
    total = received[0:8, :]
    for z in range(1, N_Z):
        total = total + received[z * 8 : z * 8 + 8, :]
    norm, curvature, g, h = (
        jnp.concatenate([total[i : i + 1], total[i + 4 : i + 5]], axis=1) for i in range(4)
    )
    step = norm / curvature
    scaled = step * g
    grown = scaled / curvature
    next_norm = (grown - 1.0) * norm
    next_curvature = step * (step * h) - grown * scaled
    next_step = next_norm / next_curvature
    both = step + next_step * grown
    cross = next_step * step
    for k in range(4):
        rows = rows_of(k)
        split_into(wide.at[:, 0 : 2 * NRHS], k, both * p()[rows, :] - cross * v()[rows, :])
    for k in range(4):
        rows = rows_of(k)
        w = halves[k]()[...] + held(halves[k + 4])[...]
        value = r()[rows, :] - both * t()[rows, :] + cross * w
        split_into(wide.at[:, 2 * NRHS : 4 * NRHS], k, value)
    for j, out in enumerate(made):
        two = mm(perm_t[...], wide[:, 2 * j * NRHS : 2 * (j + 1) * NRHS])
        out.ref[...] = two[:, :NRHS] + two[:, NRHS:]
        out.send()


PLANES = [[s * N_DEV + z * N_X + x for s in range(N_SUB) for x in range(N_X)] for z in range(N_Z)]
LINES = [[z * N_X + x for z in range(N_Z)] for x in range(N_X)]


def over_plane(v):
    return lax.all_to_all(v, ("sub", "dev"), 0, 0, tiled=True, axis_index_groups=PLANES)


def over_line(v):
    return lax.all_to_all(v, "dev", 0, 0, tiled=True, axis_index_groups=LINES)


def ring(v, axis, count, shift):
    return lax.ppermute(v, axis, [(i, (i + shift) % count) for i in range(count)])


def halo(blocks):
    return [
        ring(blocks[1], "sub", N_SUB, 1),
        ring(blocks[0], "sub", N_SUB, -1),
        ring(blocks[3], "dev", N_DEV, 1),
        ring(blocks[2], "dev", N_DEV, -1),
    ]


def together(first, *others):
    return lax.optimization_barrier((first, *others))


def small(body, outs, ins, smem=(), flops=LONG):
    return run(
        body,
        outs,
        ins,
        smem=smem,
        near=[i for i in range(len(ins)) if i not in smem],
        near_outs=range(len(outs)),
        limit=12,
        flops=flops,
    )


def shards(
    load, schur, local_inverse, coarse_basis, coarse_inverse, dof_lists, coarse_map, stiffness
):
    dof = dof_lists[0]
    block = shape(CAP, NRHS)
    vector = shape(NI, NRHS)
    square = shape(NI, NI, dtype=BF16)
    lanes = shape(NRHS, 128)
    table = shape(NI, 384, dtype=BF16)
    wide = pltpu.VMEM((NI, 2 * NRHS), BF16)
    half = pltpu.VMEM((NI, NI), BF16)
    big = 2 * NI * NI * NRHS

    *hs, weights = run(
        prepare,
        [shape(HROWS, NRHS)] * 4 + [shape(8, NRHS)],
        [dof, coarse_basis, load, coarse_map, stiffness.reshape(1, -1)],
        near_outs=range(4),
        scratch=[pltpu.VMEM((NI, 2 * NRHS + 128), BF16)],
        flops=3 * big,
    )
    gs = halo(hs)
    (schur_s,) = run(
        order, [square], [dof, schur], scratch=[half, half], limit=59, flops=8 * big
    )
    coarse_inverse, schur_s = together(coarse_inverse, schur_s)
    planes = [
        lax.ppermute(
            coarse_inverse,
            "dev",
            [(z * N_X + x, z * N_X + (x + i) % N_X) for z in range(N_Z) for x in range(N_X)],
        )
        for i in range(1, N_X)
    ]
    schur_s, *gs = together(schur_s, *gs)
    send, sent, r, placed = run(
        begin,
        [shape(PEERS * 16, 128), lanes, vector, shape(128, NI)],
        [*hs, *gs],
        near=range(8),
        near_outs=(0,),
        limit=60.2,
        scratch=[pltpu.VMEM((256, NI), BF16)],
        flops=big // 2,
    )
    (inverse_s,) = run(order, [square], [dof, local_inverse], scratch=[half, half], flops=8 * big)
    (plane,) = small(plane_rows, [shape(128, NC)], [coarse_inverse, *planes], flops=0)
    received, inverse_s, plane = together(over_plane(send), inverse_s, plane)
    line, pick = small(gather_first, [shape(N_Z * 8, NC), shape(NC, 768, dtype=BF16)], [received])

    def coarse_middle(received):
        (part,) = small(coarse_solve, [shape(N_Z * 8, 128)], [received, plane])
        return part

    def coarse_end(part):
        (back,) = small(give_back, [shape(PEERS * 8, 128)], [part, pick])
        return back

    energy, *es = run(
        begin_local,
        [shape(8, NRHS)] + [block] * 4,
        [weights, r, inverse_s],
        scratch=[wide],
        flops=2 * big,
    )
    es_halo = halo(es)
    received, energy = together(over_line(line), energy)
    part = coarse_middle(received)
    placed, *es_halo = together(placed, *es_halo)
    rows, columns, images, coarse = run(
        basis_tables,
        [shape(256, NI, dtype=BF16), table, table, shape(128, 128)],
        [placed, schur_s],
        flops=big,
    )
    received, rows, columns, images, coarse = together(
        over_line(part), rows, columns, images, coarse
    )
    back = coarse_end(received)
    local, image, send_local, other = run(
        first_middle,
        [vector, vector, lanes, shape(8, NRHS)],
        [schur_s, rows, *es, *es_halo],
        scratch=[wide],
        flops=2 * big,
    )
    solved = over_plane(back)
    (sending,) = small(first_send, [lanes], [solved, send_local, coarse])
    solved, send = together(solved, sending)
    kept, *qs = run(
        first_direction,
        [lanes] + [block] * 4,
        [solved, images, image],
        near=(0,),
        flops=big,
    )
    qs_halo = halo(qs)
    received, *qs = together(over_plane(send), *qs)
    (line,) = small(gather_again, [shape(N_Z * 8, NC)], [received, pick])
    (dots,) = run(
        first_energies, [shape(8, NRHS)], [energy, other, kept, sent, send_local, coarse]
    )
    received, dots = together(over_line(line), dots)
    part = coarse_middle(received)
    _, inverse_s = together(part, inverse_s)
    t, dots, *es = run(
        second_local,
        [vector, shape(8, NRHS)] + [block] * 4,
        [weights, *qs, *qs_halo, inverse_s, dots],
        scratch=[wide],
        flops=2 * big,
    )
    es_halo = halo(es)
    received, dots = together(over_line(part), dots)
    back = coarse_end(received)
    local_too, image, packed = run(
        second_middle,
        [vector, vector, shape(NRHS + 16, 128)],
        [schur_s, rows, dots, *es, *es_halo],
        scratch=[wide],
        flops=2 * big,
    )
    solved = over_plane(back)
    (send,) = small(dots_send, [lanes], [solved, sending, packed, coarse])
    solved, send = together(solved, send)
    kept_too, *us = run(
        second_direction,
        [lanes] + [block] * 4,
        [solved, images, image],
        near=(0,),
        flops=big,
    )
    us_halo = halo(us)
    received, *us = together(over_plane(send), *us)
    (line,) = small(add_plane, [shape(N_Z * 8, 128)], [received])
    line, local_too = together(line, local_too)
    p, v = run(
        vectors,
        [vector, vector],
        [columns, kept, local, kept_too, local_too],
        flops=big // 2,
    )
    received, p, v = together(over_line(line), p, v)
    return tuple(
        run(
            finish,
            [vector, vector],
            [received, dof, p, v, r, t, *us, *us_halo],
            near=(0, 10, 11, 12, 13),
            limit=59,
            scratch=[half, pltpu.VMEM((NI, 4 * NRHS), BF16)],
            flops=4 * big,
        )
    )


def solution(mesh):
    placed = (
        P(("sub", "dev"), None),
        P(("sub", "dev"), None),
        P(("sub", "dev"), None),
        P(("sub", "dev"), None),
        P("dev", None),
        P(("sub", "dev"), None, None),
        P(("sub", "dev"), None),
        P(),
    )
    return jax.shard_map(
        shards,
        mesh=mesh,
        in_specs=placed,
        out_specs=(P(("sub", "dev"), None), P(("sub", "dev"), None)),
        check_vma=False,
    )
```

```python
import jax
import jax.numpy as jnp
import numpy as np
from jax import lax
from jax.experimental import pallas as pl
from jax.experimental.pallas import tpu as pltpu
from jax.sharding import PartitionSpec as P

F32, BF16 = jnp.float32, jnp.bfloat16
EXACT = lax.Precision.HIGHEST
NI, NRHS, NCL, CAP, NC = 1024, 256, 16, 256, 1024
N_SUB, N_DEV, N_X, N_Z = 8, 32, 4, 8
PEERS = N_SUB * N_X
MIB = 1 << 20
LONG = 20 << 30
NN = (((1,), (0,)), ((), ()))
NT = (((1,), (1,)), ((), ()))


def mm(a, b, dims=NN, precision=None):
    return lax.dot_general(a, b, dims, precision=precision, preferred_element_type=F32)


def pieces(v, count):
    out = []
    for i in range(count):
        part = v.astype(BF16)
        out.append(part)
        if i + 1 < count:
            v = v - part.astype(F32)
    return out


def shape(*dims, dtype=F32):
    return jax.ShapeDtypeStruct(dims, dtype)


CHUNK = 256 << 10


def start_copies(source, target, arrived, rows, itemsize):
    size = int(np.prod(target.shape[1:])) * itemsize
    step = max(16, CHUNK // size // 16 * 16)
    for first in range(0, rows, step):
        at = pl.ds(first, min(step, rows - first))
        pltpu.make_async_copy(source.at[at], target.at[at], arrived).start()


class Operand:
    def __init__(self, source, target, arrived):
        self.target, self.waited = target, False
        self.copy = pltpu.make_async_copy(source, target, arrived)
        start_copies(source, target, arrived, target.shape[0], target.dtype.itemsize)

    def __call__(self):
        if not self.waited:
            self.copy.wait()
            self.waited = True
        return self.target


class Result:
    def __init__(self, source, target, arrived):
        self.ref, self.target, self.arrived, self.sent = source, target, arrived, 0
        self.copy = pltpu.make_async_copy(source, target, arrived)

    def send(self):
        if not self.sent:
            self.sent = self.ref.shape[0]
            start_copies(self.ref, self.target, self.arrived, self.sent, self.ref.dtype.itemsize)

    def send_rows(self, count):
        at = pl.ds(self.sent, count)
        pltpu.make_async_copy(self.ref.at[at], self.target.at[at], self.arrived).start()
        self.sent += count


def run(body, outs, ins, smem=(), near=(), near_outs=(), part=None, scratch=(), limit=61, flops=0):
    part = part or {}
    places = {i: pltpu.SMEM for i in smem} | {i: pltpu.VMEM for i in near}
    far = [i for i in range(len(ins)) if i not in places]
    far_outs = [i for i in range(len(outs)) if i not in near_outs]
    rows = {i: part.get(i, (0, ins[i].shape[0])) for i in far}
    buffers = [pltpu.VMEM((rows[i][1],) + ins[i].shape[1:], ins[i].dtype) for i in far]
    buffers += [pltpu.VMEM(outs[i].shape, outs[i].dtype) for i in far_outs]
    count = len(buffers)
    size = sum(int(np.prod(a.shape)) * a.dtype.itemsize for a in list(ins) + list(outs))

    def kernel(*refs):
        given, refs = list(refs[: len(ins)]), refs[len(ins) :]
        made, refs = list(refs[: len(outs)]), refs[len(outs) :]
        held, arrived, rest = refs[:count], refs[count], refs[count + 1 :]
        for n, i in enumerate(far):
            begin, length = rows[i]
            source = given[i] if length == ins[i].shape[0] else given[i].at[pl.ds(begin, length)]
            given[i] = Operand(source, held[n], arrived.at[n])
        for n, i in enumerate(far_outs, len(far)):
            made[i] = Result(held[n], made[i], arrived.at[n])
        body(given, made, *rest)
        for i in far_outs:
            made[i].send()
        for i in far:
            given[i]()
        for i in far_outs:
            made[i].copy.wait()

    return pl.pallas_call(
        kernel,
        out_shape=list(outs),
        in_specs=[pl.BlockSpec(memory_space=places.get(i, pltpu.HBM)) for i in range(len(ins))],
        out_specs=[
            pl.BlockSpec(memory_space=pltpu.VMEM if i in near_outs else pltpu.HBM)
            for i in range(len(outs))
        ],
        scratch_shapes=buffers + [pltpu.SemaphoreType.DMA((max(count, 1),))] + list(scratch),
        compiler_params=pltpu.CompilerParams(vmem_limit_bytes=int(limit * MIB)),
        cost_estimate=pl.CostEstimate(flops=flops, bytes_accessed=size, transcendentals=0),
        name=body.__name__,
    )(*ins)


def slot_weights(stiffness):
    p = lax.axis_index("sub") * N_DEV + lax.axis_index("dev")
    lanes = iota((1, NRHS), 1)

    def value(q):
        q = jnp.clip(q, 0, N_SUB * N_DEV - 1)
        one = jnp.sum(jnp.where(lanes == q, stiffness, 0.0), axis=1, keepdims=True)
        return jnp.broadcast_to(one, (1, NRHS))

    own = value(p)
    return [own / (own + value(p + shift)) for shift in (-N_DEV, N_DEV, -1, 1)]


def iota(dims, axis):
    return lax.broadcasted_iota(jnp.int32, dims, axis)


def slot_major(dof):
    wide = jnp.concatenate([dof.astype(F32), jnp.zeros((4, CAP), F32)], axis=0)
    columns = jnp.transpose(wide)
    lanes = iota((CAP, NI), 1).astype(F32)
    return (jnp.where(columns[:, k : k + 1] == lanes, 1.0, 0.0).astype(BF16) for k in range(4))


def unknown_major(dof):
    rows = iota((NI, CAP), 0)
    return [jnp.where(rows == dof[k : k + 1, :], 1.0, 0.0).astype(BF16) for k in range(4)]


def rows_of(k):
    return slice(k * CAP, (k + 1) * CAP)


HROWS = CAP + NCL + 8


def prepare(given, made, wide):
    dof, basis, load, names, stiffness = given
    *hs, weights_out = made
    blocks = slot_major(dof()[...])
    turned = jnp.transpose(jnp.concatenate([basis()[...], jnp.zeros((48, NI), F32)], axis=0))
    high, low = pieces(turned, 2)
    wide[:, 2 * NRHS : 2 * NRHS + 64] = high
    wide[:, 2 * NRHS + 64 :] = low
    for i, part in enumerate(pieces(load()[...], 2)):
        wide[:, i * NRHS : (i + 1) * NRHS] = part
    tiled = jnp.where(
        lax.rem(iota((NCL, NRHS), 1), NCL) == iota((NCL, NRHS), 0), 1.0, 0.0
    ).astype(BF16)
    ids = pieces(jnp.broadcast_to(names()[...].astype(F32), (8, NCL)), 2)
    ids = mm(ids[0], tiled) + mm(ids[1], tiled)
    weights = slot_weights(stiffness()[...])
    weights_out.ref[...] = jnp.concatenate(weights + [jnp.zeros((4, NRHS), F32)], axis=0)
    weights_out.send()
    for k, h in enumerate(hs):
        both = mm(next(blocks), wide[...])
        h[0:CAP, :] = both[:, :NRHS] + both[:, NRHS : 2 * NRHS]
        own = jnp.transpose(both[:, 2 * NRHS :])
        h[CAP : CAP + NCL, :] = weights[k] * (own[0:NCL] + own[64 : 64 + NCL])
        h[CAP + NCL :, :] = ids


def order(given, made, perm, half):
    dof, source = given
    for k, block in enumerate(slot_major(dof()[...])):
        perm[rows_of(k), :] = block
        half[rows_of(k), :] = mm(block, source()[...]).astype(BF16)
    for k in range(4):
        made[0].ref[rows_of(k), :] = mm(half[rows_of(k), :], perm[...], NT).astype(BF16)
        made[0].send_rows(CAP)


def plane_rows(given, made):
    x = lax.rem(lax.axis_index("dev"), N_X)
    for i, block in enumerate(given):
        at = lax.rem(x + (N_X - i), N_X) * 32
        made[0][pl.ds(pl.multiple_of(at, 32), 32), :] = block[...]


def block_product(matrix, wide):
    both = mm(matrix[...], wide[...])
    both = both[:, :NRHS] + both[:, NRHS:]
    return [both[rows_of(k), :] for k in range(4)]


def split_into(wide, k, v):
    for i, part in enumerate(pieces(v, 2)):
        wide[rows_of(k), i * NRHS : (i + 1) * NRHS] = part


def project(rows, k, v):
    four = mm(rows[:, rows_of(k)], jnp.concatenate(pieces(v, 2), axis=1))
    return four[:128, :NRHS] + four[:128, NRHS:] + four[128:, :NRHS]


def solved_pieces(solved):
    high, low = pieces(solved[...], 2)
    return jnp.concatenate([high, high, low], axis=1)


def lane_slot(j):
    return lax.div(iota((8, 128), 1), NCL) == j


def place_basis(hs, gs, placed):
    s = lax.axis_index("sub")
    x = lax.rem(lax.axis_index("dev"), N_X)
    odd = lax.rem(s, 2)
    own = odd * 4 + x
    across, over, edge = (
        (1 - odd) * 4 + x,
        (1 - odd) * 4 + lax.rem(x + 1, 4),
        (1 - odd) * 4 + lax.rem(x + 2, 4),
    )
    places = (
        jnp.where(odd == 1, across, over),
        jnp.where(odd == 1, over, across),
        jnp.where(x > 0, odd * 4 + x - 1, edge),
        jnp.where(x < N_X - 1, odd * 4 + x + 1, edge),
    )
    placed[...] = jnp.zeros_like(placed)
    for k in range(4):
        for at, source in ((own, hs[k]), (places[k], gs[k])):
            at = pl.ds(pl.multiple_of(at * NCL, NCL), NCL)
            placed[at, rows_of(k)] = source[CAP : CAP + NCL, :]
    return s, x, own


def fill_rows(rows, placed):
    for i, part in enumerate(pieces(placed[...], 2)):
        rows[i * 128 : (i + 1) * 128, :] = part


def lane_sum(v):
    return mm(jnp.ones((8, 128), F32), v, NT, precision=EXACT)[0:1]


def rows_out(out, rows):
    full = 8 - sum(row.shape[0] for row in rows)
    out.ref[...] = jnp.concatenate(list(rows) + [jnp.zeros((full, NRHS), F32)], axis=0)


def begin(given, made, rows):
    hs, gs = given[0:4], given[4:8]
    send, sent, r_out, placed = made
    s, x, own = place_basis(hs, gs, placed.ref)
    placed.send()
    for k in range(4):
        r_out.ref[rows_of(k), :] = hs[k][0:CAP, :] + gs[k][0:CAP, :]
        r_out.send_rows(CAP)
    fill_rows(rows, placed.ref)
    total = jnp.zeros((128, NRHS), F32)
    for k in range(4):
        total = total + project(rows, k, hs[k][0:CAP, :])
    flipped = jnp.transpose(total)
    sent.ref[...] = flipped
    sent.send()
    zero = jnp.zeros((8, 128), F32)
    line = iota((8, 128), 0)
    mine = jnp.where(lane_slot(own), hs[0][CAP + NCL :, 0:128], zero)
    before = jnp.where(lane_slot(s) & (x == 0), gs[2][CAP + NCL :, 0:128], zero)
    after = jnp.where(lane_slot(s) & (x == N_X - 1), gs[3][CAP + NCL :, 0:128], zero)
    extra = jnp.where(line == 0, mine, jnp.where(line == 1, before, jnp.where(line == 2, after, zero)))
    for m in range(PEERS):
        send[m * 16 : m * 16 + 8, :] = flipped[m * 8 : m * 8 + 8, :]
        send[m * 16 + 8 : m * 16 + 16, :] = extra


def begin_local(given, made, wide):
    weights, r, inverse = given
    energy, *es = made
    weights = weights()
    for k in range(4):
        split_into(wide, k, weights[k : k + 1, :] * r()[rows_of(k), :])
    total = jnp.zeros((1, NRHS), F32)
    for k, (e, value) in enumerate(zip(es, block_product(inverse(), wide))):
        value = weights[k : k + 1, :] * value
        e.ref[...] = value
        e.send()
        total = total + jnp.sum(value * r()[rows_of(k), :], axis=0, keepdims=True)
    rows_out(energy, [total])


def three_wide(out, v):
    high, low = pieces(v, 2)
    out[:, 0:128] = high
    out[:, 128:256] = low
    out[:, 256:384] = high


def basis_tables(given, made):
    placed, schur = given
    rows, columns, images, coarse = made
    fill_rows(rows.ref, placed())
    rows.send()
    three_wide(columns.ref, jnp.transpose(placed()[...]))
    columns.send()
    both = mm(schur()[...], columns.ref[:, 0:256])
    three_wide(images.ref, both[:, :128] + both[:, 128:])
    images.send()
    four = mm(rows.ref[...], images.ref[:, 0:256])
    coarse.ref[...] = four[:128, :128] + four[:128, 128:] + four[128:, :128]


def layout(m):
    s, x = divmod(m, N_X)
    odd = s % 2
    keep = [odd * 4 + x, (1 - odd) * 4 + x]
    keep += [odd * 4 + v for v in (x - 1, x + 1) if 0 <= v < N_X]
    moves = []
    other = s + 1 if odd else s - 1
    if 0 <= other < N_SUB:
        moves.append(((1 - odd) * 4 + (x + 1) % 4, other // 2, (1 - odd) * 4 + x))
    if x in (0, N_X - 1):
        moves.append(((1 - odd) * 4 + (x + 2) % 4, 4 if x == 0 else 5, s))
    return s // 2, keep, moves


def lanes_in(slots):
    at = lax.div(iota((8, 128), 1), NCL)
    hit = at == slots[0]
    for j in slots[1:]:
        hit = hit | (at == j)
    return hit


def roll_slots(v, shift):
    shift = (shift * NCL) % 128
    return pltpu.roll(v, shift, 1) if shift else v


def spread(tiles):
    groups = [jnp.zeros((8, 128), F32) for _ in range(6)]
    for m in range(PEERS):
        base, keep, moves = layout(m)
        tile = tiles(m)
        groups[base] = groups[base] + jnp.where(lanes_in(keep), tile, 0.0)
        for here, group, there in moves:
            part = roll_slots(jnp.where(lanes_in([here]), tile, 0.0), there - here)
            groups[group] = groups[group] + part
    return jnp.concatenate(groups, axis=1)


def fold(groups, pick, out):
    three = mm(jnp.concatenate(pieces(groups, 3), axis=0), pick, NT)
    result = three[0:8] + three[8:16] + three[16:24]
    for z in range(N_Z):
        out[z * 8 : z * 8 + 8, :] = result


def gather_first(given, made):
    received = given[0]
    out, pick_out = made
    groups = spread(lambda m: received[m * 16 : m * 16 + 8, :])
    ids = [jnp.zeros((8, 128), F32) for _ in range(6)]
    for m in range(PEERS):
        extra = received[m * 16 + 8 : m * 16 + 16, :]
        base = m // 8
        ids[base] = ids[base] + extra
        ids[4] = ids[4] + extra
        ids[5] = ids[5] + extra
    index = jnp.concatenate(
        [ids[0][0:1], ids[1][0:1], ids[2][0:1], ids[3][0:1], ids[4][1:2], ids[5][2:3]], axis=1
    ).astype(jnp.int32)
    pick = jnp.where(iota((NC, 768), 0) == index, 1.0, 0.0).astype(BF16)
    pick_out[...] = pick
    fold(groups, pick, out)


def gather_again(given, made):
    received, pick = given
    groups = spread(lambda m: received[m * 8 : m * 8 + 8, :])
    fold(groups, pick[...], made[0])


def coarse_solve(given, made):
    received, plane = given
    out = made[0]
    rhs = received[0:8, :]
    for z in range(1, N_Z):
        rhs = rhs + received[z * 8 : z * 8 + 8, :]
    solved = mm(rhs, plane[...], NT, precision=EXACT)
    for z in range(N_Z):
        out[z * 8 : z * 8 + 8, :] = solved


def give_back(given, made):
    received, pick = given
    out = made[0]
    solved = jnp.concatenate([received[z * 8 : z * 8 + 8, :] for z in range(N_Z)], axis=1)
    three = mm(jnp.concatenate(pieces(solved, 3), axis=0), pick[...])
    every = three[0:8] + three[8:16] + three[16:24]
    groups = [every[:, g * 128 : (g + 1) * 128] for g in range(6)]
    for m in range(PEERS):
        base, keep, moves = layout(m)
        tile = jnp.where(lanes_in(keep), groups[base], 0.0)
        for here, group, there in moves:
            tile = jnp.where(lanes_in([here]), roll_slots(groups[group], here - there), tile)
        out[m * 8 : m * 8 + 8, :] = tile


def middle(schur, rows, halves, local_out, image, send_local, wide):
    for k in range(4):
        local = halves[k]()[...] + halves[k + 4]()[...]
        local_out.ref[rows_of(k), :] = local
        local_out.send_rows(CAP)
        split_into(wide, k, local)
    total = jnp.zeros((128, NRHS), F32)
    energy = jnp.zeros((1, NRHS), F32)
    for k, value in enumerate(block_product(schur(), wide)):
        image.ref[rows_of(k), :] = value
        image.send_rows(CAP)
        energy = energy + jnp.sum(value * local_out.ref[rows_of(k), :], axis=0, keepdims=True)
        total = total + project(rows(), k, value)
    send_local.ref[0:NRHS, :] = jnp.transpose(total)
    return energy


def first_middle(given, made, wide):
    *halves, schur, rows = given
    local_out, image, send_local, energy = made
    rows_out(energy, [middle(schur, rows, halves, local_out, image, send_local, wide)])


def energies(solved, sent, send_local, coarse):
    cross = 2.0 * send_local + mm(solved, coarse, NT, precision=EXACT)
    return lane_sum(solved * sent), lane_sum(solved * cross)


def first_send(given, made):
    solved, send_local, coarse = given
    product = mm(solved[...], coarse[...], NT, precision=EXACT)
    made[0][...] = send_local[...] + product


def held(v):
    return v() if isinstance(v, Operand) else v


def add_coarse(given, made):
    solved, images, image = given
    kept, *outs = made
    kept.ref[...] = solved[...]
    kept.send()
    back = solved_pieces(solved)
    for k, out in enumerate(outs):
        rows = rows_of(k)
        out.ref[...] = image()[rows, :] + mm(images()[rows, :], back, NT)
        out.send()


def first_direction(given, made):
    add_coarse(given, made)


def second_direction(given, made):
    add_coarse(given, made)


def first_energies(given, made):
    energy, other, solved, sent, send_local, coarse = given
    norm, curvature = energies(solved()[...], sent()[...], send_local()[...], coarse()[...])
    rows_out(made[0], [energy()[0:1, :] + norm, other()[0:1, :] + curvature])


def second_local(given, made, wide):
    weights, *halves = given[:9]
    inverse, dots = given[9:]
    t_out, dots_out, *es = made
    weights = weights()
    for k in range(4):
        t = halves[k]()[...] + halves[k + 4]()[...]
        t_out.ref[rows_of(k), :] = t
        t_out.send_rows(CAP)
        split_into(wide, k, weights[k : k + 1, :] * t)
    total = jnp.zeros((1, NRHS), F32)
    for k, (e, value) in enumerate(zip(es, block_product(inverse(), wide))):
        value = weights[k : k + 1, :] * value
        e.ref[...] = value
        e.send()
        total = total + jnp.sum(value * t_out.ref[rows_of(k), :], axis=0, keepdims=True)
    rows_out(dots_out, [dots()[0:2, :], total])


def second_middle(given, made, wide):
    *halves, schur, rows, dots = given
    local_out, image, packed = made
    energy = middle(schur, rows, halves, local_out, image, packed, wide)
    tail = jnp.concatenate([dots()[0:3, :], energy, jnp.zeros((4, NRHS), F32)], axis=0)
    packed.ref[NRHS : NRHS + 8, :] = tail[:, 0:128]
    packed.ref[NRHS + 8 : NRHS + 16, :] = tail[:, 128:]


def dots_send(given, made):
    solved, sent, packed, coarse = given
    first, second = energies(solved[...], sent[...], packed[0:NRHS, :], coarse[...])
    dots = jnp.concatenate([packed[NRHS : NRHS + 8, :], packed[NRHS + 8 :, :]], axis=1)
    values = (dots[0:1, :], dots[1:2, :], dots[2:3, :] + first, dots[3:4, :] + second)
    tile = jnp.concatenate([v[:, :128] for v in values] + [v[:, 128:] for v in values], axis=0)
    for m in range(PEERS):
        made[0][m * 8 : m * 8 + 8, :] = tile


def add_plane(given, made):
    received, out = given[0], made[0]
    total = received[0:8, :]
    for m in range(1, PEERS):
        total = total + received[m * 8 : m * 8 + 8, :]
    for z in range(N_Z):
        out[z * 8 : z * 8 + 8, :] = total


def vectors(given, made):
    columns, solved, local, solved_too, local_too = given
    for out, back, v in ((made[0], solved, local), (made[1], solved_too, local_too)):
        back = solved_pieces(back())
        for k in range(4):
            rows = rows_of(k)
            out.ref[rows, :] = v()[rows, :] + mm(columns()[rows, :], back, NT)
            out.send_rows(CAP)


def finish(given, made, perm_t, wide):
    received, dof, p, v, r, t, *halves = given
    for k, block in enumerate(unknown_major(dof()[...])):
        perm_t[:, rows_of(k)] = block
    total = received[0:8, :]
    for z in range(1, N_Z):
        total = total + received[z * 8 : z * 8 + 8, :]
    norm, curvature, g, h = (
        jnp.concatenate([total[i : i + 1], total[i + 4 : i + 5]], axis=1) for i in range(4)
    )
    step = norm / curvature
    scaled = step * g
    grown = scaled / curvature
    next_norm = (grown - 1.0) * norm
    next_curvature = step * (step * h) - grown * scaled
    next_step = next_norm / next_curvature
    both = step + next_step * grown
    cross = next_step * step
    for k in range(4):
        rows = rows_of(k)
        split_into(wide.at[:, 0 : 2 * NRHS], k, both * p()[rows, :] - cross * v()[rows, :])
    for k in range(4):
        rows = rows_of(k)
        w = halves[k]()[...] + held(halves[k + 4])[...]
        value = r()[rows, :] - both * t()[rows, :] + cross * w
        split_into(wide.at[:, 2 * NRHS : 4 * NRHS], k, value)
    for j, out in enumerate(made):
        two = mm(perm_t[...], wide[:, 2 * j * NRHS : 2 * (j + 1) * NRHS])
        out.ref[...] = two[:, :NRHS] + two[:, NRHS:]
        out.send()


PLANES = [[s * N_DEV + z * N_X + x for s in range(N_SUB) for x in range(N_X)] for z in range(N_Z)]
LINES = [[z * N_X + x for z in range(N_Z)] for x in range(N_X)]


def over_plane(v):
    return lax.all_to_all(v, ("sub", "dev"), 0, 0, tiled=True, axis_index_groups=PLANES)


def over_line(v):
    return lax.all_to_all(v, "dev", 0, 0, tiled=True, axis_index_groups=LINES)


def ring(v, axis, count, shift):
    return lax.ppermute(v, axis, [(i, (i + shift) % count) for i in range(count)])


def halo(blocks):
    return [
        ring(blocks[1], "sub", N_SUB, 1),
        ring(blocks[0], "sub", N_SUB, -1),
        ring(blocks[3], "dev", N_DEV, 1),
        ring(blocks[2], "dev", N_DEV, -1),
    ]


def together(first, *others):
    return lax.optimization_barrier((first, *others))


def small(body, outs, ins, smem=(), flops=LONG):
    return run(
        body,
        outs,
        ins,
        smem=smem,
        near=[i for i in range(len(ins)) if i not in smem],
        near_outs=range(len(outs)),
        limit=12,
        flops=flops,
    )


def shards(
    load, schur, local_inverse, coarse_basis, coarse_inverse, dof_lists, coarse_map, stiffness
):
    dof = dof_lists[0]
    block = shape(CAP, NRHS)
    vector = shape(NI, NRHS)
    square = shape(NI, NI, dtype=BF16)
    lanes = shape(NRHS, 128)
    table = shape(NI, 384, dtype=BF16)
    wide = pltpu.VMEM((NI, 2 * NRHS), BF16)
    half = pltpu.VMEM((NI, NI), BF16)
    big = 2 * NI * NI * NRHS

    *hs, weights = run(
        prepare,
        [shape(HROWS, NRHS)] * 4 + [shape(8, NRHS)],
        [dof, coarse_basis, load, coarse_map, stiffness.reshape(1, -1)],
        near_outs=range(4),
        scratch=[pltpu.VMEM((NI, 2 * NRHS + 128), BF16)],
        flops=3 * big,
    )
    gs = halo(hs)
    (schur_s,) = run(
        order, [square], [dof, schur], scratch=[half, half], limit=59, flops=8 * big
    )
    coarse_inverse, schur_s = together(coarse_inverse, schur_s)
    planes = [
        lax.ppermute(
            coarse_inverse,
            "dev",
            [(z * N_X + x, z * N_X + (x + i) % N_X) for z in range(N_Z) for x in range(N_X)],
        )
        for i in range(1, N_X)
    ]
    schur_s, *gs = together(schur_s, *gs)
    send, sent, r, placed = run(
        begin,
        [shape(PEERS * 16, 128), lanes, vector, shape(128, NI)],
        [*hs, *gs],
        near=range(8),
        near_outs=(0,),
        limit=60.2,
        scratch=[pltpu.VMEM((256, NI), BF16)],
        flops=big // 2,
    )
    (inverse_s,) = run(order, [square], [dof, local_inverse], scratch=[half, half], flops=8 * big)
    (plane,) = small(plane_rows, [shape(128, NC)], [coarse_inverse, *planes], flops=0)
    received, inverse_s, plane = together(over_plane(send), inverse_s, plane)
    line, pick = small(gather_first, [shape(N_Z * 8, NC), shape(NC, 768, dtype=BF16)], [received])

    def coarse_middle(received):
        (part,) = small(coarse_solve, [shape(N_Z * 8, 128)], [received, plane])
        return part

    def coarse_end(part):
        (back,) = small(give_back, [shape(PEERS * 8, 128)], [part, pick])
        return back

    energy, *es = run(
        begin_local,
        [shape(8, NRHS)] + [block] * 4,
        [weights, r, inverse_s],
        scratch=[wide],
        flops=2 * big,
    )
    es_halo = halo(es)
    received, energy = together(over_line(line), energy)
    part = coarse_middle(received)
    placed, *es_halo = together(placed, *es_halo)
    rows, columns, images, coarse = run(
        basis_tables,
        [shape(256, NI, dtype=BF16), table, table, shape(128, 128)],
        [placed, schur_s],
        flops=big,
    )
    received, rows, columns, images, coarse = together(
        over_line(part), rows, columns, images, coarse
    )
    back = coarse_end(received)
    local, image, send_local, other = run(
        first_middle,
        [vector, vector, lanes, shape(8, NRHS)],
        [*es, *es_halo, schur_s, rows],
        scratch=[wide],
        flops=2 * big,
    )
    solved = over_plane(back)
    (sending,) = small(first_send, [lanes], [solved, send_local, coarse])
    solved, send = together(solved, sending)
    kept, *qs = run(
        first_direction,
        [lanes] + [block] * 4,
        [solved, images, image],
        near=(0,),
        flops=big,
    )
    qs_halo = halo(qs)
    received, *qs = together(over_plane(send), *qs)
    (line,) = small(gather_again, [shape(N_Z * 8, NC)], [received, pick])
    (dots,) = run(
        first_energies, [shape(8, NRHS)], [energy, other, kept, sent, send_local, coarse]
    )
    received, dots = together(over_line(line), dots)
    part = coarse_middle(received)
    _, inverse_s = together(part, inverse_s)
    t, dots, *es = run(
        second_local,
        [vector, shape(8, NRHS)] + [block] * 4,
        [weights, *qs, *qs_halo, inverse_s, dots],
        scratch=[wide],
        flops=2 * big,
    )
    es_halo = halo(es)
    received, dots = together(over_line(part), dots)
    back = coarse_end(received)
    local_too, image, packed = run(
        second_middle,
        [vector, vector, shape(NRHS + 16, 128)],
        [*es, *es_halo, schur_s, rows, dots],
        scratch=[wide],
        flops=2 * big,
    )
    solved = over_plane(back)
    (send,) = small(dots_send, [lanes], [solved, sending, packed, coarse])
    solved, send = together(solved, send)
    kept_too, *us = run(
        second_direction,
        [lanes] + [block] * 4,
        [solved, images, image],
        near=(0,),
        flops=big,
    )
    us_halo = halo(us)
    received, *us = together(over_plane(send), *us)
    (line,) = small(add_plane, [shape(N_Z * 8, 128)], [received])
    line, local_too = together(line, local_too)
    p, v = run(
        vectors,
        [vector, vector],
        [columns, kept, local, kept_too, local_too],
        flops=big // 2,
    )
    received, p, v = together(over_line(line), p, v)
    return tuple(
        run(
            finish,
            [vector, vector],
            [received, dof, p, v, r, t, *us, *us_halo],
            near=(0, 10, 11, 12, 13),
            limit=59,
            scratch=[half, pltpu.VMEM((NI, 4 * NRHS), BF16)],
            flops=4 * big,
        )
    )


def solution(mesh):
    placed = (
        P(("sub", "dev"), None),
        P(("sub", "dev"), None),
        P(("sub", "dev"), None),
        P(("sub", "dev"), None),
        P("dev", None),
        P(("sub", "dev"), None, None),
        P(("sub", "dev"), None),
        P(),
    )
    return jax.shard_map(
        shards,
        mesh=mesh,
        in_specs=placed,
        out_specs=(P(("sub", "dev"), None), P(("sub", "dev"), None)),
        check_vma=False,
    )
```
